256 devices in a mesh: space: 64 (over x, y_hi, z), mode: 4 (over y_lo, core).
Axes of the slice: x: 4, y: 4 (y_hi: 2, y_lo: 2; y = y_hi * 2 + y_lo), z: 8, core: 2. Of those that a mesh axis runs over, the one named last changes fastest.
Arguments:
- chaos_field: float32 [84, 64, 128, 128], P('mode', 'space'), may hold values from -6 to 6
- mean_field: float32 [64, 128, 128], P('space'), may hold values from 0.5 to 2
- kl_fields: float32 [6, 64, 128, 128], P(None, 'space'), may hold values from -1.8 to 1.8
- pattern: int32 [7, 84, 84], replicated, may hold values from 0 to 1, as said below
- coupling: float32 [7, 84, 84], replicated, as said below
- slot_mode: int32 [84], replicated, may hold values from 0 to 83, each once
Outputs:
- product: float32 [84, 64, 128, 128], P('mode', 'space')
The draws below stay inside these ranges and needn't reach their ends.
Inputs may be any that keep to these rules, and one draw needn't show every extreme that they name: Modes are the 84 multi-indices of total degree at most 3 in 6 variables; pattern[0] is the identity; each term k >= 1 belongs to one variable, each variable to one term, and pattern[k, a, b] is 1 exactly where the multi-indices of modes a and b differ by one in that variable and agree elsewhere. coupling[0] is the identity; for k >= 1, coupling[k, a, b] is the square root of the larger of the two degrees in the term's variable where pattern[k, a, b] is 1, and zero elsewhere; pattern and coupling name the same variable for each term. `slot_mode`: each slot holds a different chaos mode.
All inputs are finite; a program needn't handle non-finite values.
Results may differ from the reference program's by a relative error of at most 0.000082.
Values sent between devices are 32-bit elements; how exact they have to be, the bound alone decides.
A program may use at most 320 MiB of HBM per device.

```python
import math
import jax
import jax.numpy as jnp
import numpy as np
from jax import lax

P_SIZE = 84
KL = 6
NXY = 128
NZ = 64


def compositions(variables, degree):
    if variables == 1:
        return [(degree,)]
    listing = []
    for leading in range(degree, -1, -1):
        for remainder in compositions(variables - 1, degree - leading):
            listing.append((leading,) + remainder)
    return listing


def chaos_tables(variables, number_modes):
    indices = []
    for degree in range(0, 4):
        indices = indices + compositions(variables, degree)
    indices = indices[:number_modes]
    values = np.zeros((variables, number_modes, number_modes), np.float32)
    marks = np.zeros((variables, number_modes, number_modes), np.int32)
    for first_mode in range(number_modes):
        for second_mode in range(number_modes):
            differ = np.array(indices[first_mode]) - np.array(indices[second_mode])
            if int(np.sum(np.abs(differ))) == 1:
                variable = int(np.argmax(np.abs(differ)))
                larger = max(indices[first_mode][variable], indices[second_mode][variable])
                values[variable, first_mode, second_mode] = math.sqrt(larger)
                marks[variable, first_mode, second_mode] = 1
    return (values, marks)


def term_variables(key):
    return jax.random.permutation(jax.random.fold_in(key, 11), KL)


def draw_pattern(key, part):
    shuffle = term_variables(key)
    values, marks = chaos_tables(KL, P_SIZE)
    linear = jnp.asarray(marks)[shuffle]
    identity = jnp.eye(P_SIZE, dtype=jnp.int32)
    return jnp.concatenate([identity[None], linear], 0).astype(jnp.int32)


def draw_coupling(key, part):
    shuffle = term_variables(key)
    values, marks = chaos_tables(KL, P_SIZE)
    linear = jnp.asarray(values)[shuffle]
    identity = jnp.eye(P_SIZE, dtype=jnp.float32)
    return jnp.concatenate([identity[None], linear], 0).astype(jnp.float32)


def block_scale(rng, dims, split, low, largest):
    loudness, own = 1.0, jax.random.fold_in(rng, 6)
    for dim, shards_of in split:
        heights = jnp.exp(jax.random.uniform(jax.random.fold_in(own, dim), (shards_of,), jnp.float32, low / len(split), largest / len(split)))
        loudness = loudness * jnp.repeat(heights, dims[dim] // shards_of).reshape([-1 if axis == dim else 1 for axis in range(len(dims))])
    return loudness


def normal_values(own_key, shape, deviation, reach, pieces=(), held_as=jnp.bfloat16):
    loudness = block_scale(own_key, shape, pieces, -0.22, 0.18) if pieces else 1.0
    drawn = jax.random.normal(own_key, shape, jnp.float32) * deviation * loudness
    return jnp.minimum(jnp.maximum(drawn, -reach), reach).astype(held_as)


def setup_inputs(seed: int = 0) -> dict:
    keys = jax.random.split(jax.random.key(seed), 7)
    chaos_field = normal_values(keys[0], (P_SIZE, NZ, NXY, NXY), 1.0, 6.0, ((0, 4), (1, 64)), jnp.float32)
    mean_field = jnp.clip(jnp.exp(math.log(2.0) - 1.3862944 * jax.random.uniform(keys[1], (NZ, NXY, NXY), jnp.float32) ** block_scale(keys[1], (NZ, NXY, NXY), ((0, 64),), -0.2, 0.2)), 0.5, 2.0)
    kl_fields = normal_values(keys[2], (KL, NZ, NXY, NXY), 0.3, 1.8, ((1, 64),), jnp.float32)
    pattern = draw_pattern(jax.random.fold_in(keys[6], 71), 0)
    coupling = draw_coupling(jax.random.fold_in(keys[6], 71), 0)
    slot_mode = jax.random.permutation(keys[5], P_SIZE).astype(jnp.int32)
    return dict(chaos_field=chaos_field, mean_field=mean_field, kl_fields=kl_fields, pattern=pattern, coupling=coupling, slot_mode=slot_mode)


def face_weights(coef_ext):
    coef_here = coef_ext[:, 1:-1]
    height = coef_here.shape[2]
    breadth = coef_here.shape[3]
    coef_pad = jnp.pad(coef_here, ((0, 0), (0, 0), (1, 1), (1, 1)))
    weights = [0.5 * (coef_here + coef_ext[:, 2:]), 0.5 * (coef_here + coef_ext[:, :-2])]
    for shift_y, shift_x in ((2, 1), (0, 1), (1, 2), (1, 0)):
        weights.append(0.5 * (coef_here + coef_pad[:, :, shift_y:shift_y + height, shift_x:shift_x + breadth]))
    diagonal = weights[0] + weights[1] + weights[2] + weights[3] + weights[4] + weights[5]
    return diagonal, weights


def apply_operator(coef_ext, field_ext):
    diagonal, weights = face_weights(coef_ext)
    field_here = field_ext[:, 1:-1]
    height = field_here.shape[2]
    breadth = field_here.shape[3]
    field_pad = jnp.pad(field_here, ((0, 0), (0, 0), (1, 1), (1, 1)))
    total = diagonal * field_here - weights[0] * field_ext[:, 2:] - weights[1] * field_ext[:, :-2]
    index = 2
    for shift_y, shift_x in ((2, 1), (0, 1), (1, 2), (1, 0)):
        total = total - weights[index] * field_pad[:, :, shift_y:shift_y + height, shift_x:shift_x + breadth]
        index = index + 1
    return total


def slot_coupling(pattern, coupling, slot_mode):
    masked = coupling * pattern.astype(jnp.float32)
    return masked[:, slot_mode][:, :, slot_mode]


def reference(chaos_field, mean_field, kl_fields, pattern, coupling, slot_mode):
    coupled = slot_coupling(pattern, coupling, slot_mode)
    coefs = jnp.concatenate([mean_field[None], kl_fields], 0)
    coef_ext = jnp.pad(coefs, ((0, 0), (1, 1), (0, 0), (0, 0)))

    def one_slot(slot):
        weights = lax.dynamic_index_in_dim(coupled, slot, 1, keepdims=False)
        mixed = jnp.einsum('kt,tzyx->kzyx', weights, chaos_field, precision=lax.Precision.HIGHEST)
        mixed_ext = jnp.pad(mixed, ((0, 0), (1, 1), (0, 0), (0, 0)))
        return jnp.sum(apply_operator(coef_ext, mixed_ext), axis=0)

    return lax.map(one_slot, jnp.arange(P_SIZE, dtype=jnp.int32))
```

```python
import jax
import jax.numpy as jnp
from jax import lax
from jax.experimental import pallas as pl
from jax.experimental.pallas import tpu as pltpu
from jax.sharding import PartitionSpec as P

MESH = pl.DeviceIdType.MESH
RING = 8
GROUPS = 4
QUOTA = 21
SLOTS = GROUPS * QUOTA
TERMS = 7
ROWS = 8
PAD = 24
DEPTH = 176
SIDE = 128
CHUNKS = SIDE // ROWS
PAIRS = CHUNKS // 2
F32 = jnp.float32
BF16 = jnp.bfloat16


def split(value):
    high = value.astype(BF16)
    return high, (value - high.astype(F32)).astype(BF16)


def dot(left, right):
    return jnp.dot(left, right, preferred_element_type=F32)


def iota(shape, dim):
    return lax.broadcasted_iota(jnp.int32, shape, dim)


def over_pad(index):
    return (index * 43691) >> 20


def build_mixing(groups, pattern, coupling, slots, mixing):
    of_mode = (iota((SLOTS, SLOTS), 0) == slots[...]).astype(BF16)
    row, col = iota((GROUPS * PAD, SLOTS), 0), iota((GROUPS * PAD, SLOTS), 1)
    part = over_pad(row)
    inner = row - part * PAD
    pick = ((col == part * QUOTA + inner) & (inner < QUOTA)).astype(BF16)
    left = lax.dot_general(
        pick, of_mode, (((1,), (1,)), ((), ())), preferred_element_type=F32
    ).astype(BF16)
    row, col = iota((SLOTS, DEPTH), 0), iota((SLOTS, DEPTH), 1)
    part = over_pad(col)
    inner = col - part * PAD
    rights = []
    for group in groups:
        pick = ((row == group * QUOTA + inner) & (inner < QUOTA)).astype(BF16)
        rights.append(dot(of_mode, pick).astype(BF16))
    term = over_pad(iota((GROUPS * PAD, DEPTH), 1))
    totals = [[jnp.zeros((GROUPS * PAD, DEPTH), F32)] * 2 for _ in groups]
    for k in range(TERMS):
        masked = coupling[k] * pattern[k].astype(F32)
        for level, part in enumerate(split(masked)):
            rows = dot(left, part).astype(BF16)
            for i, right in enumerate(rights):
                totals[i][level] = jnp.where(term == k, dot(rows, right), totals[i][level])
    for i in range(len(groups)):
        for level in range(2):
            mixing[i, level] = totals[i][level].astype(BF16)


def mix(mixing, i, values):
    high, low = split(values)
    return (
        dot(mixing[i, 0], high) + dot(mixing[i, 1], high) + dot(mixing[i, 0], low)
    )


def slots_inside(block):
    zeros = jnp.zeros((PAD - QUOTA, ROWS, SIDE), F32)
    return jnp.swapaxes(jnp.concatenate([block, zeros], 0), 0, 1)


def kernel(
    u_hbm, mean_hbm, kl_hbm, pattern_hbm, coupling_hbm, slots_hbm, own_out, far_out,
    field, turned, coef, pattern, coupling, slots, mixing, halo, edge, weight, centre, partial, near,
    load_sem, store_sem,
    halo_send, halo_recv, edge_send, edge_recv, pass_send, pass_recv, near_send, near_recv, far_send, far_recv,
):
    place = lax.axis_index("space")
    mode = lax.axis_index("mode")
    planes = lax.axis_size("space")
    core = mode % 2
    sibling = mode + 1 - 2 * core
    across = (mode + 2) % 4
    diagonal = (sibling + 2) % 4
    along = place % RING
    mode_up = jnp.where(along == RING - 1, across, mode)
    mode_down = jnp.where(along == 0, across, mode)
    has_up = place < planes - 1
    has_down = place > 0
    up = (place + 1, mode_up)
    down = (place - 1, mode_down)
    sends = ((has_up, up), (has_down, down))
    comes = (has_down, has_up)

    loads = [
        pltpu.make_async_copy(u_hbm.at[:, 0], field, load_sem.at[0]),
        pltpu.make_async_copy(mean_hbm, coef.at[pl.ds(0, 1), pl.ds(ROWS, SIDE)], load_sem.at[1]),
        pltpu.make_async_copy(kl_hbm.at[:, 0], coef.at[pl.ds(1, TERMS - 1), pl.ds(ROWS, SIDE)], load_sem.at[2]),
        pltpu.make_async_copy(pattern_hbm, pattern, load_sem.at[3]),
        pltpu.make_async_copy(coupling_hbm, coupling, load_sem.at[4]),
        pltpu.make_async_copy(slots_hbm, slots, load_sem.at[5]),
    ]
    for i in (1, 2, 0, 3, 4, 5):
        loads[i].start()

    barrier = pltpu.get_barrier_semaphore()

    def greet(device):
        pl.semaphore_signal(barrier, inc=1, device_id=device, device_id_type=MESH)

    for there, device in sends:
        pl.when(there)(lambda device=device: greet(device))
    greet((place, sibling))
    greet((place, across))

    zero_rows = jnp.zeros((TERMS, ROWS, SIDE), F32)
    coef[:, pl.ds(0, ROWS)] = zero_rows
    coef[:, pl.ds(ROWS + SIDE, ROWS)] = zero_rows
    turned[0] = jnp.zeros((PAD, SIDE), F32)
    turned[SIDE + 1] = jnp.zeros((PAD, SIDE), F32)

    for h in range(2):

        @pl.when(jnp.logical_not(comes[h]))
        def _():
            @pl.loop(0, CHUNKS)
            def _(j):
                halo[h, j] = jnp.zeros((QUOTA, ROWS, SIDE), F32)
                edge[h, j] = zero_rows

    loads[1].wait()
    loads[2].wait()
    pl.semaphore_wait(barrier, 2 + has_up.astype(jnp.int32) + has_down.astype(jnp.int32))

    def halo_copy(h, j):
        return pltpu.make_async_remote_copy(
            src_ref=u_hbm.at[:, 0, pl.ds(pl.multiple_of(j * ROWS, ROWS), ROWS)],
            dst_ref=halo.at[h, j],
            send_sem=halo_send.at[h, j],
            recv_sem=halo_recv.at[h, j],
            device_id=sends[h][1],
            device_id_type=MESH,
        )

    def edge_copy(h, p):
        j = 2 * p + core
        return pltpu.make_async_remote_copy(
            src_ref=coef.at[:, pl.ds(pl.multiple_of(ROWS + j * ROWS, ROWS), ROWS)],
            dst_ref=edge.at[h, j],
            send_sem=edge_send.at[h, p],
            recv_sem=edge_recv.at[h, p],
            device_id=sends[h][1],
            device_id_type=MESH,
        )

    def pass_copy(h, p, mine):
        j = 2 * p + (core if mine else 1 - core)
        return pltpu.make_async_remote_copy(
            src_ref=edge.at[h, j],
            dst_ref=edge.at[h, j],
            send_sem=pass_send.at[h, p],
            recv_sem=pass_recv.at[h, p],
            device_id=(place, sibling),
            device_id_type=MESH,
        )

    def near_copy(i, j):
        return pltpu.make_async_remote_copy(
            src_ref=partial.at[j, (sibling, diagonal)[i]],
            dst_ref=near.at[j, i],
            send_sem=near_send.at[i, j],
            recv_sem=near_recv.at[i, j],
            device_id=(place, sibling),
            device_id_type=MESH,
        )

    def rows_of(j):
        return pl.ds(pl.multiple_of(j * ROWS, ROWS), ROWS)

    def far_copy(j):
        return pltpu.make_async_remote_copy(
            src_ref=partial.at[j, across],
            dst_ref=far_out.at[:, rows_of(j)],
            send_sem=far_send.at[j],
            recv_sem=far_recv.at[j],
            device_id=(place, across),
            device_id_type=MESH,
        )

    def own_copy(j):
        return pltpu.make_async_copy(partial.at[j, mode], own_out.at[:, rows_of(j)], store_sem.at[j])

    for h in range(2):
        pl.when(sends[h][0])(lambda h=h: edge_copy(h, 0).start())

    @pl.loop(0, PAIRS)
    def _(p):
        for h in range(2):

            @pl.when(sends[h][0])
            def _():
                @pl.when(p < PAIRS - 1)
                def _():
                    edge_copy(h, p + 1).start()

                halo_copy(h, 2 * p).start()

        for h in range(2):
            pl.when(sends[h][0])(lambda h=h: halo_copy(h, 2 * p + 1).start())

    loads[3].wait()
    loads[4].wait()
    loads[5].wait()
    build_mixing((mode, mode_down, mode_up), pattern, coupling, slots, mixing)
    loads[0].wait()

    @pl.loop(0, CHUNKS)
    def _(j):
        turned[pl.ds(j * ROWS + 1, ROWS)] = slots_inside(field[:, rows_of(j)])

    def relay_edges(p):
        for h in range(2):

            @pl.when(comes[h])
            def _():
                edge_copy(h, p).wait_recv()
                pass_copy(h, p, True).start()

    def take_edges(p):
        for h in range(2):
            pl.when(comes[h])(lambda h=h: pass_copy(h, p, False).wait_recv())

    first = iota((1, 1, SIDE), 2) == 0
    last = iota((1, 1, SIDE), 2) == SIDE - 1

    def own_part(j):
        block = coef[:, pl.ds(pl.multiple_of(j * ROWS, ROWS), 3 * ROWS)]
        here = block[:, ROWS : 2 * ROWS]
        right = 0.5 * (here + jnp.where(last, 0.0, pltpu.roll(here, SIDE - 1, 2)))
        left = 0.5 * (here + jnp.where(first, 0.0, pltpu.roll(here, 1, 2)))
        after = 0.5 * (here + block[:, ROWS + 1 : 2 * ROWS + 1])
        before = 0.5 * (here + block[:, ROWS - 1 : 2 * ROWS - 1])
        below = 0.5 * (here + edge[0, j])
        above = 0.5 * (here + edge[1, j])
        weight[0] = right + left + after + before + below + above
        weight[1] = jnp.where(last, 0.0, -right)
        weight[2] = jnp.where(first, 0.0, -left)
        weight[3] = -after
        weight[4] = -before
        weight[5] = -below
        weight[6] = -above
        for r in range(0, ROWS, 2):
            sides = []
            for q in (r, r + 1):
                y = j * ROWS + q + 1
                own = turned[y]
                values = (own, pltpu.roll(own, SIDE - 1, 1), pltpu.roll(own, 1, 1), turned[y + 1], turned[y - 1])
                terms = []
                for k in range(TERMS):
                    total = weight[0, k, q : q + 1] * values[0]
                    for i in range(1, 5):
                        total = total + weight[i, k, q : q + 1] * values[i]
                    terms.append(total)
                sides.append(jnp.concatenate(terms + [jnp.zeros((DEPTH - TERMS * PAD, SIDE), F32)], 0))
            mixed = mix(mixing, 0, jnp.concatenate(sides, 1))
            centre[r] = mixed[:, :SIDE]
            centre[r + 1] = mixed[:, SIDE:]

    def halo_part(j):
        for h in range(2):
            pl.when(comes[h])(lambda h=h: halo_copy(h, j).wait_recv())
        beside = [slots_inside(halo[h, j]) for h in range(2)]
        results = []
        for r in range(0, ROWS, 2):
            mixed = jnp.concatenate([centre[r], centre[r + 1]], 1)
            for h in range(2):
                sides = []
                for q in (r, r + 1):
                    terms = [weight[5 + h, k, q : q + 1] * beside[h][q] for k in range(TERMS)]
                    sides.append(jnp.concatenate(terms + [jnp.zeros((DEPTH - TERMS * PAD, SIDE), F32)], 0))
                mixed = mixed + mix(mixing, 1 + h, jnp.concatenate(sides, 1))
            results.extend([mixed[None, :, :SIDE], mixed[None, :, SIDE:]])
        by_slot = jnp.swapaxes(jnp.concatenate(results, 0), 0, 1)
        for g in range(GROUPS):
            partial[j, g] = by_slot[g * PAD : g * PAD + QUOTA]
        near_copy(1, j).start()
        near_copy(0, j).start()

    def join(j):
        near_copy(1, j).wait_recv()
        partial[j, across] = partial[j, across] + near[j, 1]
        far_copy(j).start()
        near_copy(0, j).wait_recv()
        partial[j, mode] = partial[j, mode] + near[j, 0]
        own_copy(j).start()

    relay_edges(0)
    take_edges(0)
    own_part(0)

    @pl.loop(0, PAIRS)
    def _(p):
        halo_part(2 * p)
        pl.when(p < PAIRS - 1)(lambda: relay_edges(p + 1))
        own_part(2 * p + 1)
        join(2 * p)
        halo_part(2 * p + 1)

        @pl.when(p < PAIRS - 1)
        def _():
            take_edges(p + 1)
            own_part(2 * p + 2)

        join(2 * p + 1)

    @pl.loop(0, PAIRS)
    def _(p):
        for h in range(2):

            @pl.when(sends[h][0])
            def _():
                edge_copy(h, p).wait_send()
                halo_copy(h, 2 * p).wait_send()
                halo_copy(h, 2 * p + 1).wait_send()

            pl.when(comes[h])(lambda h=h: pass_copy(h, p, True).wait_send())

    @pl.loop(0, CHUNKS)
    def _(j):
        for i in range(2):
            near_copy(i, j).wait_send()
        far_copy(j).wait()
        own_copy(j).wait()


def on_device(chaos_field, mean_field, kl_fields, pattern, coupling, slot_mode):
    dma = pltpu.SemaphoreType.DMA
    result = pltpu.VMEM((QUOTA, SIDE, SIDE), F32)
    operands = (chaos_field, mean_field, kl_fields, pattern, coupling, slot_mode.reshape(1, SLOTS))
    operands = [pltpu.with_memory_space_constraint(operand, pltpu.HBM) for operand in operands]
    own, far = pl.pallas_call(
        kernel,
        out_shape=(result, result),
        in_specs=[pl.BlockSpec(memory_space=pltpu.HBM)] * len(operands),
        out_specs=(pl.BlockSpec(memory_space=pl.ANY),) * 2,
        scratch_shapes=[
            pltpu.VMEM((QUOTA, SIDE, SIDE), F32),
            pltpu.VMEM((SIDE + 2, PAD, SIDE), F32),
            pltpu.VMEM((TERMS, SIDE + 2 * ROWS, SIDE), F32),
            pltpu.VMEM((TERMS, SLOTS, SLOTS), jnp.int32),
            pltpu.VMEM((TERMS, SLOTS, SLOTS), F32),
            pltpu.VMEM((1, SLOTS), jnp.int32),
            pltpu.VMEM((3, 2, GROUPS * PAD, DEPTH), BF16),
            pltpu.VMEM((2, CHUNKS, QUOTA, ROWS, SIDE), F32),
            pltpu.VMEM((2, CHUNKS, TERMS, ROWS, SIDE), F32),
            pltpu.VMEM((7, TERMS, ROWS, SIDE), F32),
            pltpu.VMEM((ROWS, GROUPS * PAD, SIDE), F32),
            pltpu.VMEM((CHUNKS, GROUPS, QUOTA, ROWS, SIDE), F32),
            pltpu.VMEM((CHUNKS, 2, QUOTA, ROWS, SIDE), F32),
            dma((6,)),
            dma((CHUNKS,)),
            dma((2, CHUNKS)),
            dma((2, CHUNKS)),
            dma((2, PAIRS)),
            dma((2, PAIRS)),
            dma((2, PAIRS)),
            dma((2, PAIRS)),
            dma((2, CHUNKS)),
            dma((2, CHUNKS)),
            dma((CHUNKS,)),
            dma((CHUNKS,)),
        ],
        compiler_params=pltpu.CompilerParams(
            collective_id=0, has_side_effects=True, vmem_limit_bytes=40 << 20
        ),
    )(*operands)
    return (own + far).reshape(QUOTA, 1, SIDE, SIDE)


def solution(mesh):
    in_specs = (
        P("mode", "space", None, None),
        P("space", None, None),
        P(None, "space", None, None),
        P(),
        P(),
        P(),
    )
    out_specs = P("mode", "space", None, None)
    return jax.shard_map(
        on_device, mesh=mesh, in_specs=in_specs, out_specs=out_specs, check_vma=False
    )
```

```python
import jax
import jax.numpy as jnp
from jax import lax
from jax.experimental import pallas as pl
from jax.experimental.pallas import tpu as pltpu
from jax.sharding import PartitionSpec as P

MESH = pl.DeviceIdType.MESH
RING = 8
GROUPS = 4
QUOTA = 21
SLOTS = GROUPS * QUOTA
TERMS = 7
ROWS = 8
PAD = 24
DEPTH = 176
SIDE = 128
CHUNKS = SIDE // ROWS
PAIRS = CHUNKS // 2
LATE = 4
EARLY = CHUNKS - LATE
LOOPS = EARLY // 2
GATHERED = LATE + 1
DENSE = 256
MIXED = GROUPS * PAD
F32 = jnp.float32
BF16 = jnp.bfloat16


def split(value):
    high = value.astype(BF16)
    return high, (value - high.astype(F32)).astype(BF16)


def dot(left, right):
    return jnp.dot(left, right, preferred_element_type=F32)


def iota(shape, dim):
    return lax.broadcasted_iota(jnp.int32, shape, dim)


def over_pad(index):
    return (index * 43691) >> 20


def build_mixing(groups, pattern, coupling, slots, mixing, turned_mixing):
    of_mode = (iota((SLOTS, SLOTS), 0) == slots[...]).astype(BF16)
    row, col = iota((MIXED, SLOTS), 0), iota((MIXED, SLOTS), 1)
    part = over_pad(row)
    inner = row - part * PAD
    pick = ((col == part * QUOTA + inner) & (inner < QUOTA)).astype(BF16)
    left = lax.dot_general(
        pick, of_mode, (((1,), (1,)), ((), ())), preferred_element_type=F32
    ).astype(BF16)
    row, col = iota((MIXED, DENSE), 0), iota((MIXED, DENSE), 1)
    part = over_pad(row)
    inner = row - part * PAD
    again = (col >= SLOTS).astype(jnp.int32) + (col >= 2 * SLOTS).astype(jnp.int32)
    dense = (col - again * SLOTS == part * QUOTA + inner) & (inner < QUOTA)
    dense = [(dense & (again < 2)).astype(BF16), (dense & (again == 2)).astype(BF16)]
    row, col = iota((SLOTS, DEPTH), 0), iota((SLOTS, DEPTH), 1)
    part = over_pad(col)
    inner = col - part * PAD
    rights = []
    for group in groups:
        pick = ((row == group * QUOTA + inner) & (inner < QUOTA)).astype(BF16)
        rights.append(dot(of_mode, pick).astype(BF16))
    term = over_pad(iota((MIXED, DEPTH), 1))
    totals = [[jnp.zeros((MIXED, DEPTH), F32)] * 2 for _ in groups]
    for k in range(TERMS):
        masked = coupling[k] * pattern[k].astype(F32)
        for level, part in enumerate(split(masked)):
            rows = dot(left, part).astype(BF16)
            for i, right in enumerate(rights):
                totals[i][level] = jnp.where(term == k, dot(rows, right), totals[i][level])
    for i in range(len(groups)):
        turned = jnp.zeros((DEPTH, DENSE), F32)
        for level in range(2):
            matrix = totals[i][level].astype(BF16)
            mixing[i, level * MIXED : (level + 1) * MIXED] = matrix
            turned = turned + lax.dot_general(
                matrix, dense[level], (((0,), (0,)), ((), ())), preferred_element_type=F32
            )
        turned_mixing[i] = turned.astype(BF16)


def mix(mixing, i, values):
    high, low = split(values)
    both = dot(mixing[i], high)
    return both[:MIXED] + both[MIXED:] + dot(mixing[i, :MIXED], low)


def slots_inside(block):
    zeros = jnp.zeros((PAD - QUOTA, ROWS, SIDE), F32)
    return jnp.swapaxes(jnp.concatenate([block, zeros], 0), 0, 1)


def kernel(
    u_hbm, mean_hbm, kl_hbm, pattern_hbm, coupling_hbm, slots_hbm, own_out, far_out,
    field, turned, coef, pattern, coupling, slots, mixing, turned_mixing, halo, edge, weight, centre, partial, near,
    gathered, dense, mixed_rows, blank,
    load_sem, store_sem, blank_sem,
    gather_send, gather_recv,
    halo_send, halo_recv, edge_send, edge_recv, pass_send, pass_recv, near_send, near_recv, far_send, far_recv,
):
    place = lax.axis_index("space")
    mode = lax.axis_index("mode")
    planes = lax.axis_size("space")
    core = mode % 2
    sibling = mode + 1 - 2 * core
    across = (mode + 2) % 4
    diagonal = (sibling + 2) % 4
    along = place % RING
    mode_up = jnp.where(along == RING - 1, across, mode)
    mode_down = jnp.where(along == 0, across, mode)
    has_up = place < planes - 1
    has_down = place > 0
    up = (place + 1, mode_up)
    down = (place - 1, mode_down)
    sends = ((has_up, up), (has_down, down))
    comes = (has_down, has_up)

    loads = [
        pltpu.make_async_copy(u_hbm.at[:, 0], field, load_sem.at[0]),
        pltpu.make_async_copy(mean_hbm, coef.at[pl.ds(0, 1), pl.ds(ROWS, SIDE)], load_sem.at[1]),
        pltpu.make_async_copy(kl_hbm.at[:, 0], coef.at[pl.ds(1, TERMS - 1), pl.ds(ROWS, SIDE)], load_sem.at[2]),
        pltpu.make_async_copy(pattern_hbm, pattern, load_sem.at[3]),
        pltpu.make_async_copy(coupling_hbm, coupling, load_sem.at[4]),
        pltpu.make_async_copy(slots_hbm, slots, load_sem.at[5]),
    ]
    for i in (1, 2, 0, 3, 4, 5):
        loads[i].start()

    barrier = pltpu.get_barrier_semaphore()

    def greet(device):
        pl.semaphore_signal(barrier, inc=1, device_id=device, device_id_type=MESH)

    for there, device in sends:
        pl.when(there)(lambda device=device: greet(device))
    greet((place, sibling))
    greet((place, across))

    zero_rows = jnp.zeros((TERMS, ROWS, SIDE), F32)
    coef[:, pl.ds(0, ROWS)] = zero_rows
    coef[:, pl.ds(ROWS + SIDE, ROWS)] = zero_rows
    turned[0] = jnp.zeros((PAD, SIDE), F32)
    turned[SIDE + 1] = jnp.zeros((PAD, SIDE), F32)

    for h in range(2):

        @pl.when(jnp.logical_not(comes[h]))
        def _():
            @pl.loop(0, CHUNKS)
            def _(j):
                halo[h, j] = jnp.zeros((QUOTA, ROWS, SIDE), F32)
                edge[h, j] = zero_rows

    loads[1].wait()
    loads[2].wait()
    pl.semaphore_wait(barrier, 2 + has_up.astype(jnp.int32) + has_down.astype(jnp.int32))

    def halo_copy(h, j):
        return pltpu.make_async_remote_copy(
            src_ref=u_hbm.at[:, 0, pl.ds(pl.multiple_of(j * ROWS, ROWS), ROWS)],
            dst_ref=halo.at[h, j],
            send_sem=halo_send.at[h, j],
            recv_sem=halo_recv.at[h, j],
            device_id=sends[h][1],
            device_id_type=MESH,
        )

    def edge_copy(h, p):
        j = 2 * p + core
        return pltpu.make_async_remote_copy(
            src_ref=coef.at[:, pl.ds(pl.multiple_of(ROWS + j * ROWS, ROWS), ROWS)],
            dst_ref=edge.at[h, j],
            send_sem=edge_send.at[h, p],
            recv_sem=edge_recv.at[h, p],
            device_id=sends[h][1],
            device_id_type=MESH,
        )

    def pass_copy(h, p, mine):
        j = 2 * p + (core if mine else 1 - core)
        return pltpu.make_async_remote_copy(
            src_ref=edge.at[h, j],
            dst_ref=edge.at[h, j],
            send_sem=pass_send.at[h, p],
            recv_sem=pass_recv.at[h, p],
            device_id=(place, sibling),
            device_id_type=MESH,
        )

    def near_copy(i, j):
        return pltpu.make_async_remote_copy(
            src_ref=partial.at[j, (sibling, diagonal)[i]],
            dst_ref=near.at[j, i],
            send_sem=near_send.at[i, j],
            recv_sem=near_recv.at[i, j],
            device_id=(place, sibling),
            device_id_type=MESH,
        )

    def rows_of(j):
        return pl.ds(pl.multiple_of(j * ROWS, ROWS), ROWS)

    def far_copy(j):
        return pltpu.make_async_remote_copy(
            src_ref=partial.at[j, across],
            dst_ref=far_out.at[:, rows_of(j)],
            send_sem=far_send.at[j],
            recv_sem=far_recv.at[j],
            device_id=(place, across),
            device_id_type=MESH,
        )

    def own_copy(j):
        return pltpu.make_async_copy(partial.at[j, mode], own_out.at[:, rows_of(j)], store_sem.at[j])

    def send_edges(p):
        for h in range(2):
            pl.when(sends[h][0])(lambda h=h: edge_copy(h, p).start())

    def gather_copy(i, c):
        rows = pl.ds(pl.multiple_of((EARLY - 1 + c) * ROWS, ROWS), ROWS)
        group = (mode, mode, across)[i]
        return pltpu.make_async_remote_copy(
            src_ref=gathered.at[c, group] if i == 2 else u_hbm.at[:, 0, rows],
            dst_ref=gathered.at[c, group],
            send_sem=gather_send.at[i, c],
            recv_sem=gather_recv.at[i, c],
            device_id=(place, (across, sibling, sibling)[i]),
            device_id_type=MESH,
        )

    def late_copy(h, c):
        return pltpu.make_async_remote_copy(
            src_ref=partial.at[EARLY + c, h],
            dst_ref=halo.at[h, EARLY + c],
            send_sem=halo_send.at[h, EARLY + c],
            recv_sem=halo_recv.at[h, EARLY + c],
            device_id=sends[h][1],
            device_id_type=MESH,
        )

    send_edges(0)

    @pl.loop(0, LOOPS)
    def _(p):
        pl.when(p < LOOPS - 1)(lambda: send_edges(p + 1))
        pl.when((p == 1) | (p == 2))(lambda: send_edges(LOOPS + p - 1))
        for j in (2 * p, 2 * p + 1):
            for h in range(2):
                pl.when(sends[h][0])(lambda h=h, j=j: halo_copy(h, j).start())

    @pl.loop(0, GATHERED)
    def _(c):
        gather_copy(0, c).start()
        gather_copy(1, c).start()

    blank[...] = jnp.zeros_like(blank)
    blank_copy = pltpu.make_async_copy(blank, far_out.at[:, pl.ds(EARLY * ROWS, LATE * ROWS)], blank_sem)
    blank_copy.start()
    dense[GATHERED * ROWS] = jnp.zeros((DENSE, SIDE), BF16)

    loads[3].wait()
    loads[4].wait()
    loads[5].wait()
    build_mixing((mode, mode_down, mode_up), pattern, coupling, slots, mixing, turned_mixing)
    loads[0].wait()

    @pl.loop(0, CHUNKS)
    def _(j):
        turned[pl.ds(j * ROWS + 1, ROWS)] = slots_inside(field[:, rows_of(j)])

    def relay_edges(p):
        for h in range(2):

            @pl.when(comes[h])
            def _():
                edge_copy(h, p).wait_recv()
                pass_copy(h, p, True).start()

    def take_edges(p):
        for h in range(2):
            pl.when(comes[h])(lambda h=h: pass_copy(h, p, False).wait_recv())

    first = iota((1, 1, SIDE), 2) == 0
    last = iota((1, 1, SIDE), 2) == SIDE - 1

    def set_weights(slot, j):
        block = coef[:, pl.ds(pl.multiple_of(j * ROWS, ROWS), 3 * ROWS)]
        here = block[:, ROWS : 2 * ROWS]
        right = 0.5 * (here + jnp.where(last, 0.0, pltpu.roll(here, SIDE - 1, 2)))
        left = 0.5 * (here + jnp.where(first, 0.0, pltpu.roll(here, 1, 2)))
        after = 0.5 * (here + block[:, ROWS + 1 : 2 * ROWS + 1])
        before = 0.5 * (here + block[:, ROWS - 1 : 2 * ROWS - 1])
        below = 0.5 * (here + edge[0, j])
        above = 0.5 * (here + edge[1, j])
        weight[slot, 0] = right + left + after + before + below + above
        weight[slot, 1] = jnp.where(last, 0.0, -right)
        weight[slot, 2] = jnp.where(first, 0.0, -left)
        weight[slot, 3] = -after
        weight[slot, 4] = -before
        weight[slot, 5] = -below
        weight[slot, 6] = -above

    def own_part(j):
        set_weights(0, j)
        for r in range(0, ROWS, 2):
            sides = []
            for q in (r, r + 1):
                y = j * ROWS + q + 1
                own = turned[y]
                values = (own, pltpu.roll(own, SIDE - 1, 1), pltpu.roll(own, 1, 1), turned[y + 1], turned[y - 1])
                terms = []
                for k in range(TERMS):
                    total = weight[0, 0, k, q : q + 1] * values[0]
                    for i in range(1, 5):
                        total = total + weight[0, i, k, q : q + 1] * values[i]
                    terms.append(total)
                sides.append(jnp.concatenate(terms + [jnp.zeros((DEPTH - TERMS * PAD, SIDE), F32)], 0))
            mixed = mix(mixing, 0, jnp.concatenate(sides, 1))
            centre[r] = mixed[:, :SIDE]
            centre[r + 1] = mixed[:, SIDE:]

    def halo_part(j):
        for h in range(2):
            pl.when(comes[h])(lambda h=h: halo_copy(h, j).wait_recv())
        beside = [slots_inside(halo[h, j]) for h in range(2)]
        results = []
        for r in range(0, ROWS, 2):
            mixed = jnp.concatenate([centre[r], centre[r + 1]], 1)
            for h in range(2):
                sides = []
                for q in (r, r + 1):
                    terms = [weight[0, 5 + h, k, q : q + 1] * beside[h][q] for k in range(TERMS)]
                    sides.append(jnp.concatenate(terms + [jnp.zeros((DEPTH - TERMS * PAD, SIDE), F32)], 0))
                mixed = mixed + mix(mixing, 1 + h, jnp.concatenate(sides, 1))
            results.extend([mixed[None, :, :SIDE], mixed[None, :, SIDE:]])
        by_slot = jnp.swapaxes(jnp.concatenate(results, 0), 0, 1)
        for g in range(GROUPS):
            partial[j, g] = by_slot[g * PAD : g * PAD + QUOTA]
        near_copy(1, j).start()
        near_copy(0, j).start()

    def join(j):
        near_copy(1, j).wait_recv()
        partial[j, across] = partial[j, across] + near[j, 1]
        far_copy(j).start()
        near_copy(0, j).wait_recv()
        partial[j, mode] = partial[j, mode] + near[j, 0]
        own_copy(j).start()

    at_end = (along == 0) | (along == RING - 1)
    other = jnp.where(along == 0, 1, 2)
    used = (jnp.where(along == RING - 1, 1, 0), jnp.where(along == 0, 1, 0))

    def pass_gathered(c):
        gather_copy(0, c).wait_recv()
        gather_copy(2, c).start()

    def turn_gathered(c):
        gather_copy(1, c).wait_recv()
        gather_copy(2, c).wait_recv()
        rows = pl.ds(pl.multiple_of((EARLY - 1 + c) * ROWS, ROWS), ROWS)
        gathered[c, mode] = field[:, rows]
        block = gathered[c].reshape(SLOTS, ROWS, SIDE)
        high = block.astype(BF16).astype(F32)
        zeros = jnp.zeros((DENSE - 3 * SLOTS, ROWS, SIDE), F32)
        block = jnp.concatenate([high, block - high, high, zeros], 0)
        dense[pl.ds(c * ROWS, ROWS)] = jnp.swapaxes(block, 0, 1).astype(BF16)

    def mix_rows(slot, i, c):
        for r in range(0, ROWS + 2, 2):
            y = c * ROWS + ROWS - 1 + r
            mixed = dot(turned_mixing[i], jnp.concatenate([dense[y], dense[y + 1]], 1))
            mixed_rows[slot, r] = mixed[:, :SIDE]
            mixed_rows[slot, r + 1] = mixed[:, SIDE:]

    def by_slot(rows):
        return jnp.swapaxes(jnp.concatenate([row[None] for row in rows], 0), 0, 1)[:QUOTA]

    def late_part(c):
        set_weights(1, EARLY + c)
        mix_rows(0, 0, c)
        pl.when(at_end)(lambda: mix_rows(1, other, c))

        def term(slot, r, k):
            return mixed_rows[slot, r + 1, k * PAD : (k + 1) * PAD]

        for h in range(2):
            rows = []
            for r in range(ROWS):
                total = weight[1, 6 - h, 0, r : r + 1] * term(used[h], r, 0)
                for k in range(1, TERMS):
                    total = total + weight[1, 6 - h, k, r : r + 1] * term(used[h], r, k)
                rows.append(total)
            partial[EARLY + c, h] = by_slot(rows)
            pl.when(sends[h][0])(lambda h=h: late_copy(h, c).start())
        rows = []
        for r in range(ROWS):
            total = jnp.zeros((PAD, SIDE), F32)
            for k in range(TERMS):
                own = term(0, r, k)
                values = (own, pltpu.roll(own, SIDE - 1, 1), pltpu.roll(own, 1, 1), term(0, r + 1, k), term(0, r - 1, k))
                for i in range(5):
                    total = total + weight[1, i, k, r : r + 1] * values[i]
            rows.append(total)
        partial[EARLY + c, 2] = by_slot(rows)

    def late_join(c):
        j = EARLY + c
        for h in range(2):
            pl.when(comes[h])(lambda h=h: late_copy(h, c).wait_recv())
        partial[j, 2] = partial[j, 2] + halo[0, j] + halo[1, j]
        late_store(c).start()

    def late_store(c):
        j = EARLY + c
        return pltpu.make_async_copy(partial.at[j, 2], own_out.at[:, rows_of(j)], store_sem.at[j])

    relay_edges(0)
    take_edges(0)
    own_part(0)

    @pl.loop(0, LOOPS)
    def _(p):
        extra = (p == 1) | (p == 2)
        halo_part(2 * p)
        pl.when(p < LOOPS - 1)(lambda: relay_edges(p + 1))
        pl.when(extra)(lambda: relay_edges(LOOPS + p - 1))
        own_part(2 * p + 1)
        join(2 * p)

        @pl.when(p == 0)
        def _():
            pass_gathered(0)
            pass_gathered(1)

        @pl.when(p == 1)
        def _():
            pass_gathered(3)

        halo_part(2 * p + 1)

        @pl.when(p < LOOPS - 1)
        def _():
            take_edges(p + 1)
            own_part(2 * p + 2)

        pl.when(extra)(lambda: take_edges(LOOPS + p - 1))
        join(2 * p + 1)
        pl.when(p == 0)(lambda: pass_gathered(2))

        @pl.when(p == 1)
        def _():
            pass_gathered(4)
            pl.loop(0, GATHERED)(turn_gathered)

        pl.when((p == 2) | (p == 3))(lambda: pl.loop(2 * p - 4, 2 * p - 2)(late_part))

    pl.loop(0, LATE)(late_join)

    @pl.loop(0, PAIRS)
    def _(p):
        for h in range(2):
            pl.when(sends[h][0])(lambda h=h: edge_copy(h, p).wait_send())
            pl.when(comes[h])(lambda h=h: pass_copy(h, p, True).wait_send())

    @pl.loop(0, GATHERED)
    def _(c):
        for i in range(3):
            gather_copy(i, c).wait_send()

    @pl.loop(0, LATE)
    def _(c):
        for h in range(2):
            pl.when(sends[h][0])(lambda h=h: late_copy(h, c).wait_send())
        late_store(c).wait()

    @pl.loop(0, EARLY)
    def _(j):
        for h in range(2):
            pl.when(sends[h][0])(lambda h=h: halo_copy(h, j).wait_send())
        for i in range(2):
            near_copy(i, j).wait_send()
        own_copy(j).wait()
        far_copy(j).wait()

    blank_copy.wait()


def on_device(chaos_field, mean_field, kl_fields, pattern, coupling, slot_mode):
    dma = pltpu.SemaphoreType.DMA
    result = pltpu.VMEM((QUOTA, SIDE, SIDE), F32)
    operands = (chaos_field, mean_field, kl_fields, pattern, coupling, slot_mode.reshape(1, SLOTS))
    operands = [pltpu.with_memory_space_constraint(operand, pltpu.HBM) for operand in operands]
    own, far = pl.pallas_call(
        kernel,
        out_shape=(result, result),
        in_specs=[pl.BlockSpec(memory_space=pltpu.HBM)] * len(operands),
        out_specs=(pl.BlockSpec(memory_space=pl.ANY),) * 2,
        scratch_shapes=[
            pltpu.VMEM((QUOTA, SIDE, SIDE), F32),
            pltpu.VMEM((SIDE + 2, PAD, SIDE), F32),
            pltpu.VMEM((TERMS, SIDE + 2 * ROWS, SIDE), F32),
            pltpu.VMEM((TERMS, SLOTS, SLOTS), jnp.int32),
            pltpu.VMEM((TERMS, SLOTS, SLOTS), F32),
            pltpu.VMEM((1, SLOTS), jnp.int32),
            pltpu.VMEM((3, 2 * MIXED, DEPTH), BF16),
            pltpu.VMEM((3, DEPTH, DENSE), BF16),
            pltpu.VMEM((2, CHUNKS, QUOTA, ROWS, SIDE), F32),
            pltpu.VMEM((2, CHUNKS, TERMS, ROWS, SIDE), F32),
            pltpu.VMEM((2, 7, TERMS, ROWS, SIDE), F32),
            pltpu.VMEM((ROWS, MIXED, SIDE), F32),
            pltpu.VMEM((CHUNKS, GROUPS, QUOTA, ROWS, SIDE), F32),
            pltpu.VMEM((EARLY, 2, QUOTA, ROWS, SIDE), F32),
            pltpu.VMEM((GATHERED, GROUPS, QUOTA, ROWS, SIDE), F32),
            pltpu.VMEM((GATHERED * ROWS + 1, DENSE, SIDE), BF16),
            pltpu.VMEM((2, ROWS + 2, DEPTH, SIDE), F32),
            pltpu.VMEM((QUOTA, LATE * ROWS, SIDE), F32),
            dma((6,)),
            dma((CHUNKS,)),
            dma,
            dma((3, GATHERED)),
            dma((3, GATHERED)),
            dma((2, CHUNKS)),
            dma((2, CHUNKS)),
            dma((2, PAIRS)),
            dma((2, PAIRS)),
            dma((2, PAIRS)),
            dma((2, PAIRS)),
            dma((2, CHUNKS)),
            dma((2, CHUNKS)),
            dma((CHUNKS,)),
            dma((CHUNKS,)),
        ],
        compiler_params=pltpu.CompilerParams(
            collective_id=0, has_side_effects=True, vmem_limit_bytes=48 << 20
        ),
    )(*operands)
    return (own + far).reshape(QUOTA, 1, SIDE, SIDE)


def solution(mesh):
    in_specs = (
        P("mode", "space", None, None),
        P("space", None, None),
        P(None, "space", None, None),
        P(),
        P(),
        P(),
    )
    out_specs = P("mode", "space", None, None)
    return jax.shard_map(
        on_device, mesh=mesh, in_specs=in_specs, out_specs=out_specs, check_vma=False
    )
```

```python
import jax
import jax.numpy as jnp
from jax import lax
from jax.experimental import pallas as pl
from jax.experimental.pallas import tpu as pltpu
from jax.sharding import PartitionSpec as P

MESH = pl.DeviceIdType.MESH
RING = 8
GROUPS = 4
QUOTA = 21
SLOTS = GROUPS * QUOTA
TERMS = 7
ROWS = 8
PAD = 24
DEPTH = 176
SIDE = 128
CHUNKS = SIDE // ROWS
PAIRS = CHUNKS // 2
LATE = 4
EARLY = CHUNKS - LATE
LOOPS = EARLY // 2
GATHERED = LATE + 1
DENSE = 256
MIXED = GROUPS * PAD
F32 = jnp.float32
BF16 = jnp.bfloat16


def split(value):
    high = value.astype(BF16)
    return high, (value - high.astype(F32)).astype(BF16)


def dot(left, right):
    return jnp.dot(left, right, preferred_element_type=F32)


def iota(shape, dim):
    return lax.broadcasted_iota(jnp.int32, shape, dim)


def over_pad(index):
    return (index * 43691) >> 20


def build_mixing(groups, pattern, coupling, slots, mixing, turned_mixing):
    of_mode = (iota((SLOTS, SLOTS), 0) == slots[...]).astype(BF16)
    row, col = iota((MIXED, SLOTS), 0), iota((MIXED, SLOTS), 1)
    part = over_pad(row)
    inner = row - part * PAD
    pick = ((col == part * QUOTA + inner) & (inner < QUOTA)).astype(BF16)
    left = lax.dot_general(
        pick, of_mode, (((1,), (1,)), ((), ())), preferred_element_type=F32
    ).astype(BF16)
    row, col = iota((MIXED, DENSE), 0), iota((MIXED, DENSE), 1)
    part = over_pad(row)
    inner = row - part * PAD
    again = (col >= SLOTS).astype(jnp.int32) + (col >= 2 * SLOTS).astype(jnp.int32)
    dense = (col - again * SLOTS == part * QUOTA + inner) & (inner < QUOTA)
    dense = [(dense & (again < 2)).astype(BF16), (dense & (again == 2)).astype(BF16)]
    row, col = iota((SLOTS, DEPTH), 0), iota((SLOTS, DEPTH), 1)
    part = over_pad(col)
    inner = col - part * PAD
    rights = []
    for group in groups:
        pick = ((row == group * QUOTA + inner) & (inner < QUOTA)).astype(BF16)
        rights.append(dot(of_mode, pick).astype(BF16))
    term = over_pad(iota((MIXED, DEPTH), 1))
    totals = [[jnp.zeros((MIXED, DEPTH), F32)] * 2 for _ in groups]
    for k in range(TERMS):
        masked = coupling[k] * pattern[k].astype(F32)
        for level, part in enumerate(split(masked)):
            rows = dot(left, part).astype(BF16)
            for i, right in enumerate(rights):
                totals[i][level] = jnp.where(term == k, dot(rows, right), totals[i][level])
    for i in range(len(groups)):
        turned = jnp.zeros((DEPTH, DENSE), F32)
        for level in range(2):
            matrix = totals[i][level].astype(BF16)
            mixing[i, level * MIXED : (level + 1) * MIXED] = matrix
            turned = turned + lax.dot_general(
                matrix, dense[level], (((0,), (0,)), ((), ())), preferred_element_type=F32
            )
        turned_mixing[i] = turned.astype(BF16)


def mix(mixing, i, values):
    high, low = split(values)
    both = dot(mixing[i], high)
    return both[:MIXED] + both[MIXED:] + dot(mixing[i, :MIXED], low)


def slots_inside(block):
    zeros = jnp.zeros((PAD - QUOTA, ROWS, SIDE), F32)
    return jnp.swapaxes(jnp.concatenate([block, zeros], 0), 0, 1)


def kernel(
    u_hbm, mean_hbm, kl_hbm, pattern_hbm, coupling_hbm, slots_hbm, own_out, far_out,
    field, turned, coef, pattern, coupling, slots, mixing, turned_mixing, halo, edge, weight, centre, partial, near,
    gathered, dense, mixed_rows, blank,
    load_sem, store_sem, blank_sem,
    gather_send, gather_recv,
    halo_send, halo_recv, edge_send, edge_recv, pass_send, pass_recv, near_send, near_recv, far_send, far_recv,
):
    place = lax.axis_index("space")
    mode = lax.axis_index("mode")
    planes = lax.axis_size("space")
    core = mode % 2
    sibling = mode + 1 - 2 * core
    across = (mode + 2) % 4
    diagonal = (sibling + 2) % 4
    along = place % RING
    mode_up = jnp.where(along == RING - 1, across, mode)
    mode_down = jnp.where(along == 0, across, mode)
    has_up = place < planes - 1
    has_down = place > 0
    up = (place + 1, mode_up)
    down = (place - 1, mode_down)
    sends = ((has_up, up), (has_down, down))
    comes = (has_down, has_up)

    loads = [
        pltpu.make_async_copy(u_hbm.at[:, 0], field, load_sem.at[0]),
        pltpu.make_async_copy(mean_hbm, coef.at[pl.ds(0, 1), pl.ds(ROWS, SIDE)], load_sem.at[1]),
        pltpu.make_async_copy(kl_hbm.at[:, 0], coef.at[pl.ds(1, TERMS - 1), pl.ds(ROWS, SIDE)], load_sem.at[2]),
        pltpu.make_async_copy(pattern_hbm, pattern, load_sem.at[3]),
        pltpu.make_async_copy(coupling_hbm, coupling, load_sem.at[4]),
        pltpu.make_async_copy(slots_hbm, slots, load_sem.at[5]),
    ]
    for i in (1, 2, 0, 3, 4, 5):
        loads[i].start()

    barrier = pltpu.get_barrier_semaphore()

    def greet(device):
        pl.semaphore_signal(barrier, inc=1, device_id=device, device_id_type=MESH)

    for there, device in sends:
        pl.when(there)(lambda device=device: greet(device))
    greet((place, sibling))
    greet((place, across))

    zero_rows = jnp.zeros((TERMS, ROWS, SIDE), F32)
    coef[:, pl.ds(0, ROWS)] = zero_rows
    coef[:, pl.ds(ROWS + SIDE, ROWS)] = zero_rows
    turned[0] = jnp.zeros((PAD, SIDE), F32)
    turned[SIDE + 1] = jnp.zeros((PAD, SIDE), F32)

    for h in range(2):

        @pl.when(jnp.logical_not(comes[h]))
        def _():
            @pl.loop(0, CHUNKS)
            def _(j):
                halo[h, j] = jnp.zeros((QUOTA, ROWS, SIDE), F32)
                edge[h, j] = zero_rows

    loads[1].wait()
    loads[2].wait()
    pl.semaphore_wait(barrier, 2 + has_up.astype(jnp.int32) + has_down.astype(jnp.int32))

    def rows_of(j):
        return pl.ds(pl.multiple_of(j * ROWS, ROWS), ROWS)

    def halo_copy(h, j):
        return pltpu.make_async_remote_copy(
            src_ref=u_hbm.at[:, 0, pl.ds(pl.multiple_of(j * ROWS, ROWS), ROWS)],
            dst_ref=halo.at[h, j],
            send_sem=halo_send.at[h, j],
            recv_sem=halo_recv.at[h, j],
            device_id=sends[h][1],
            device_id_type=MESH,
        )

    def edge_copy(h, p):
        j = 2 * p + core
        return pltpu.make_async_remote_copy(
            src_ref=coef.at[:, pl.ds(pl.multiple_of(ROWS + j * ROWS, ROWS), ROWS)],
            dst_ref=edge.at[h, j],
            send_sem=edge_send.at[h, p],
            recv_sem=edge_recv.at[h, p],
            device_id=sends[h][1],
            device_id_type=MESH,
        )

    def pass_copy(h, p, mine):
        j = 2 * p + (core if mine else 1 - core)
        return pltpu.make_async_remote_copy(
            src_ref=edge.at[h, j],
            dst_ref=edge.at[h, j],
            send_sem=pass_send.at[h, p],
            recv_sem=pass_recv.at[h, p],
            device_id=(place, sibling),
            device_id_type=MESH,
        )

    def near_copy(i, j):
        return pltpu.make_async_remote_copy(
            src_ref=partial.at[j, (sibling, diagonal)[i]],
            dst_ref=near.at[j, i],
            send_sem=near_send.at[i, j],
            recv_sem=near_recv.at[i, j],
            device_id=(place, sibling),
            device_id_type=MESH,
        )

    def far_copy(j):
        return pltpu.make_async_remote_copy(
            src_ref=partial.at[j, across],
            dst_ref=far_out.at[:, rows_of(j)],
            send_sem=far_send.at[j],
            recv_sem=far_recv.at[j],
            device_id=(place, across),
            device_id_type=MESH,
        )

    def own_copy(j):
        return pltpu.make_async_copy(partial.at[j, mode], own_out.at[:, rows_of(j)], store_sem.at[j])

    def send_edges(p):
        for h in range(2):
            pl.when(sends[h][0])(lambda h=h: edge_copy(h, p).start())

    def gather_copy(i, c):
        rows = pl.ds(pl.multiple_of((EARLY - 1 + c) * ROWS, ROWS), ROWS)
        group = (mode, mode, across)[i]
        return pltpu.make_async_remote_copy(
            src_ref=gathered.at[c, group] if i == 2 else u_hbm.at[:, 0, rows],
            dst_ref=gathered.at[c, group],
            send_sem=gather_send.at[i, c],
            recv_sem=gather_recv.at[i, c],
            device_id=(place, (across, sibling, sibling)[i]),
            device_id_type=MESH,
        )

    def late_copy(h, c):
        return pltpu.make_async_remote_copy(
            src_ref=partial.at[EARLY + c, h],
            dst_ref=halo.at[1, EARLY + c] if h == 1 else far_out.at[:, rows_of(EARLY + c)],
            send_sem=halo_send.at[h, EARLY + c],
            recv_sem=halo_recv.at[h, EARLY + c],
            device_id=sends[h][1],
            device_id_type=MESH,
        )

    send_edges(0)

    @pl.loop(0, LOOPS)
    def _(p):
        pl.when(p < LOOPS - 1)(lambda: send_edges(p + 1))
        pl.when((p == 1) | (p == 2))(lambda: send_edges(LOOPS + p - 1))
        for j in (2 * p, 2 * p + 1):
            for h in range(2):
                pl.when(sends[h][0])(lambda h=h, j=j: halo_copy(h, j).start())

    @pl.loop(0, GATHERED)
    def _(c):
        gather_copy(0, c).start()
        gather_copy(1, c).start()

    blank_copy = pltpu.make_async_copy(blank, far_out.at[:, pl.ds(EARLY * ROWS, LATE * ROWS)], blank_sem)

    @pl.when(jnp.logical_not(has_down))
    def _():
        blank[...] = jnp.zeros_like(blank)
        blank_copy.start()

    dense[GATHERED * ROWS] = jnp.zeros((DENSE, SIDE), BF16)

    loads[3].wait()
    loads[4].wait()
    loads[5].wait()
    build_mixing((mode, mode_down, mode_up), pattern, coupling, slots, mixing, turned_mixing)
    loads[0].wait()

    @pl.loop(0, CHUNKS)
    def _(j):
        turned[pl.ds(j * ROWS + 1, ROWS)] = slots_inside(field[:, rows_of(j)])

    def relay_edges(p):
        for h in range(2):

            @pl.when(comes[h])
            def _():
                edge_copy(h, p).wait_recv()
                pass_copy(h, p, True).start()

    def take_edges(p):
        for h in range(2):
            pl.when(comes[h])(lambda h=h: pass_copy(h, p, False).wait_recv())

    first = iota((1, 1, SIDE), 2) == 0
    last = iota((1, 1, SIDE), 2) == SIDE - 1

    def set_weights(slot, j):
        block = coef[:, pl.ds(pl.multiple_of(j * ROWS, ROWS), 3 * ROWS)]
        here = block[:, ROWS : 2 * ROWS]
        right = 0.5 * (here + jnp.where(last, 0.0, pltpu.roll(here, SIDE - 1, 2)))
        left = 0.5 * (here + jnp.where(first, 0.0, pltpu.roll(here, 1, 2)))
        after = 0.5 * (here + block[:, ROWS + 1 : 2 * ROWS + 1])
        before = 0.5 * (here + block[:, ROWS - 1 : 2 * ROWS - 1])
        below = 0.5 * (here + edge[0, j])
        above = 0.5 * (here + edge[1, j])
        weight[slot, 0] = right + left + after + before + below + above
        weight[slot, 1] = jnp.where(last, 0.0, -right)
        weight[slot, 2] = jnp.where(first, 0.0, -left)
        weight[slot, 3] = -after
        weight[slot, 4] = -before
        weight[slot, 5] = -below
        weight[slot, 6] = -above

    def own_part(j):
        set_weights(0, j)
        for r in range(0, ROWS, 2):
            sides = []
            for q in (r, r + 1):
                y = j * ROWS + q + 1
                own = turned[y]
                values = (own, pltpu.roll(own, SIDE - 1, 1), pltpu.roll(own, 1, 1), turned[y + 1], turned[y - 1])
                terms = []
                for k in range(TERMS):
                    total = weight[0, 0, k, q : q + 1] * values[0]
                    for i in range(1, 5):
                        total = total + weight[0, i, k, q : q + 1] * values[i]
                    terms.append(total)
                sides.append(jnp.concatenate(terms + [jnp.zeros((DEPTH - TERMS * PAD, SIDE), F32)], 0))
            mixed = mix(mixing, 0, jnp.concatenate(sides, 1))
            centre[r] = mixed[:, :SIDE]
            centre[r + 1] = mixed[:, SIDE:]

    def halo_part(j):
        for h in range(2):
            pl.when(comes[h])(lambda h=h: halo_copy(h, j).wait_recv())
        beside = [slots_inside(halo[h, j]) for h in range(2)]
        results = []
        for r in range(0, ROWS, 2):
            mixed = jnp.concatenate([centre[r], centre[r + 1]], 1)
            for h in range(2):
                sides = []
                for q in (r, r + 1):
                    terms = [weight[0, 5 + h, k, q : q + 1] * beside[h][q] for k in range(TERMS)]
                    sides.append(jnp.concatenate(terms + [jnp.zeros((DEPTH - TERMS * PAD, SIDE), F32)], 0))
                mixed = mixed + mix(mixing, 1 + h, jnp.concatenate(sides, 1))
            results.extend([mixed[None, :, :SIDE], mixed[None, :, SIDE:]])
        by_slot = jnp.swapaxes(jnp.concatenate(results, 0), 0, 1)
        for g in range(GROUPS):
            partial[j, g] = by_slot[g * PAD : g * PAD + QUOTA]
        near_copy(1, j).start()
        near_copy(0, j).start()

    def join(j):
        near_copy(1, j).wait_recv()
        partial[j, across] = partial[j, across] + near[j, 1]
        far_copy(j).start()
        near_copy(0, j).wait_recv()
        partial[j, mode] = partial[j, mode] + near[j, 0]
        own_copy(j).start()

    at_end = (along == 0) | (along == RING - 1)
    other = jnp.where(along == 0, 1, 2)
    used = (jnp.where(along == RING - 1, 1, 0), jnp.where(along == 0, 1, 0))

    def pass_gathered(c):
        gather_copy(0, c).wait_recv()
        gather_copy(2, c).start()

    def turn_gathered(c):
        gather_copy(1, c).wait_recv()
        gather_copy(2, c).wait_recv()
        rows = pl.ds(pl.multiple_of((EARLY - 1 + c) * ROWS, ROWS), ROWS)
        gathered[c, mode] = field[:, rows]
        block = gathered[c].reshape(SLOTS, ROWS, SIDE)
        high = block.astype(BF16).astype(F32)
        zeros = jnp.zeros((DENSE - 3 * SLOTS, ROWS, SIDE), F32)
        block = jnp.concatenate([high, block - high, high, zeros], 0)
        dense[pl.ds(c * ROWS, ROWS)] = jnp.swapaxes(block, 0, 1).astype(BF16)

    def mix_rows(slot, i, c):
        for r in range(0, ROWS + 2, 2):
            y = c * ROWS + ROWS - 1 + r
            mixed = dot(turned_mixing[i], jnp.concatenate([dense[y], dense[y + 1]], 1))
            mixed_rows[slot, r] = mixed[:, :SIDE]
            mixed_rows[slot, r + 1] = mixed[:, SIDE:]

    def by_slot(rows):
        return jnp.swapaxes(jnp.concatenate([row[None] for row in rows], 0), 0, 1)[:QUOTA]

    def late_part(c):
        set_weights(1, EARLY + c)
        mix_rows(0, 0, c)
        pl.when(at_end)(lambda: mix_rows(1, other, c))

        def term(slot, r, k):
            return mixed_rows[slot, r + 1, k * PAD : (k + 1) * PAD]

        for h in range(2):
            rows = []
            for r in range(ROWS):
                total = weight[1, 6 - h, 0, r : r + 1] * term(used[h], r, 0)
                for k in range(1, TERMS):
                    total = total + weight[1, 6 - h, k, r : r + 1] * term(used[h], r, k)
                rows.append(total)
            partial[EARLY + c, h] = by_slot(rows)
            pl.when(sends[h][0])(lambda h=h: late_copy(h, c).start())
        rows = []
        for r in range(ROWS):
            total = jnp.zeros((PAD, SIDE), F32)
            for k in range(TERMS):
                own = term(0, r, k)
                values = (own, pltpu.roll(own, SIDE - 1, 1), pltpu.roll(own, 1, 1), term(0, r + 1, k), term(0, r - 1, k))
                for i in range(5):
                    total = total + weight[1, i, k, r : r + 1] * values[i]
            rows.append(total)
        partial[EARLY + c, 2] = by_slot(rows)

    def late_join(c):
        j = EARLY + c
        pl.when(has_up)(lambda: late_copy(1, c).wait_recv())
        partial[j, 2] = partial[j, 2] + halo[1, j]
        late_store(c).start()

    def late_store(c):
        j = EARLY + c
        return pltpu.make_async_copy(partial.at[j, 2], own_out.at[:, rows_of(j)], store_sem.at[j])

    relay_edges(0)
    take_edges(0)
    own_part(0)

    @pl.loop(0, LOOPS)
    def _(p):
        extra = (p == 1) | (p == 2)
        late = (p == 2) | (p == 3)
        halo_part(2 * p)
        pl.when(p < LOOPS - 1)(lambda: relay_edges(p + 1))
        pl.when(extra)(lambda: relay_edges(LOOPS + p - 1))
        own_part(2 * p + 1)
        pl.when(late)(lambda: late_part(2 * p - 4))
        join(2 * p)

        @pl.when(p == 0)
        def _():
            pass_gathered(0)
            pass_gathered(1)

        @pl.when(p == 1)
        def _():
            pass_gathered(3)

        halo_part(2 * p + 1)

        @pl.when(p < LOOPS - 1)
        def _():
            take_edges(p + 1)
            own_part(2 * p + 2)

        pl.when(extra)(lambda: take_edges(LOOPS + p - 1))
        pl.when(late)(lambda: late_part(2 * p - 3))
        join(2 * p + 1)
        pl.when(p == 0)(lambda: pass_gathered(2))

        @pl.when(p == 1)
        def _():
            pass_gathered(4)
            pl.loop(0, GATHERED)(turn_gathered)


    @pl.loop(0, PAIRS)
    def _(p):
        for h in range(2):
            pl.when(sends[h][0])(lambda h=h: edge_copy(h, p).wait_send())
            pl.when(comes[h])(lambda h=h: pass_copy(h, p, True).wait_send())

    @pl.loop(0, GATHERED)
    def _(c):
        for i in range(3):
            gather_copy(i, c).wait_send()

    @pl.loop(0, EARLY)
    def _(j):
        for h in range(2):
            pl.when(sends[h][0])(lambda h=h: halo_copy(h, j).wait_send())
        for i in range(2):
            near_copy(i, j).wait_send()

    pl.when(jnp.logical_not(has_down))(blank_copy.wait)

    pl.loop(0, LATE)(late_join)

    @pl.loop(0, EARLY)
    def _(j):
        own_copy(j).wait()
        far_copy(j).wait()

    @pl.loop(0, LATE)
    def _(c):
        for h in range(2):
            pl.when(sends[h][0])(lambda h=h: late_copy(h, c).wait_send())
        late_store(c).wait()
        pl.when(has_down)(lambda: late_copy(0, c).wait_recv())


def on_device(chaos_field, mean_field, kl_fields, pattern, coupling, slot_mode):
    dma = pltpu.SemaphoreType.DMA
    result = pltpu.VMEM((QUOTA, SIDE, SIDE), F32)
    operands = (chaos_field, mean_field, kl_fields, pattern, coupling, slot_mode.reshape(1, SLOTS))
    operands = [pltpu.with_memory_space_constraint(operand, pltpu.HBM) for operand in operands]
    own, far = pl.pallas_call(
        kernel,
        out_shape=(result, result),
        in_specs=[pl.BlockSpec(memory_space=pltpu.HBM)] * len(operands),
        out_specs=(pl.BlockSpec(memory_space=pl.ANY),) * 2,
        scratch_shapes=[
            pltpu.VMEM((QUOTA, SIDE, SIDE), F32),
            pltpu.VMEM((SIDE + 2, PAD, SIDE), F32),
            pltpu.VMEM((TERMS, SIDE + 2 * ROWS, SIDE), F32),
            pltpu.VMEM((TERMS, SLOTS, SLOTS), jnp.int32),
            pltpu.VMEM((TERMS, SLOTS, SLOTS), F32),
            pltpu.VMEM((1, SLOTS), jnp.int32),
            pltpu.VMEM((3, 2 * MIXED, DEPTH), BF16),
            pltpu.VMEM((3, DEPTH, DENSE), BF16),
            pltpu.VMEM((2, CHUNKS, QUOTA, ROWS, SIDE), F32),
            pltpu.VMEM((2, CHUNKS, TERMS, ROWS, SIDE), F32),
            pltpu.VMEM((2, 7, TERMS, ROWS, SIDE), F32),
            pltpu.VMEM((ROWS, MIXED, SIDE), F32),
            pltpu.VMEM((CHUNKS, GROUPS, QUOTA, ROWS, SIDE), F32),
            pltpu.VMEM((EARLY, 2, QUOTA, ROWS, SIDE), F32),
            pltpu.VMEM((GATHERED, GROUPS, QUOTA, ROWS, SIDE), F32),
            pltpu.VMEM((GATHERED * ROWS + 1, DENSE, SIDE), BF16),
            pltpu.VMEM((2, ROWS + 2, DEPTH, SIDE), F32),
            pltpu.VMEM((QUOTA, LATE * ROWS, SIDE), F32),
            dma((6,)),
            dma((CHUNKS,)),
            dma,
            dma((3, GATHERED)),
            dma((3, GATHERED)),
            dma((2, CHUNKS)),
            dma((2, CHUNKS)),
            dma((2, PAIRS)),
            dma((2, PAIRS)),
            dma((2, PAIRS)),
            dma((2, PAIRS)),
            dma((2, CHUNKS)),
            dma((2, CHUNKS)),
            dma((CHUNKS,)),
            dma((CHUNKS,)),
        ],
        compiler_params=pltpu.CompilerParams(
            collective_id=0, has_side_effects=True, vmem_limit_bytes=48 << 20
        ),
    )(*operands)
    return (own + far).reshape(QUOTA, 1, SIDE, SIDE)


def solution(mesh):
    in_specs = (
        P("mode", "space", None, None),
        P("space", None, None),
        P(None, "space", None, None),
        P(),
        P(),
        P(),
    )
    out_specs = P("mode", "space", None, None)
    return jax.shard_map(
        on_device, mesh=mesh, in_specs=in_specs, out_specs=out_specs, check_vma=False
    )
```

```python
import jax
import jax.numpy as jnp
from jax import lax
from jax.experimental import pallas as pl
from jax.experimental.pallas import tpu as pltpu
from jax.sharding import PartitionSpec as P

MESH = pl.DeviceIdType.MESH
RING = 8
GROUPS = 4
QUOTA = 21
SLOTS = GROUPS * QUOTA
TERMS = 7
ROWS = 8
PAD = 24
DEPTH = 176
SIDE = 128
CHUNKS = SIDE // ROWS
PAIRS = CHUNKS // 2
LATE = 4
EARLY = CHUNKS - LATE
LOOPS = EARLY // 2
GATHERED = LATE + 1
DENSE = 256
MIXED = GROUPS * PAD
F32 = jnp.float32
BF16 = jnp.bfloat16


def split(value):
    high = value.astype(BF16)
    return high, (value - high.astype(F32)).astype(BF16)


def dot(left, right):
    return jnp.dot(left, right, preferred_element_type=F32)


def iota(shape, dim):
    return lax.broadcasted_iota(jnp.int32, shape, dim)


def over_pad(index):
    return (index * 43691) >> 20


def build_mixing(groups, pattern, coupling, slots, mixing, turned_mixing):
    of_mode = (iota((SLOTS, SLOTS), 0) == slots[...]).astype(BF16)
    row, col = iota((MIXED, SLOTS), 0), iota((MIXED, SLOTS), 1)
    part = over_pad(row)
    inner = row - part * PAD
    pick = ((col == part * QUOTA + inner) & (inner < QUOTA)).astype(BF16)
    left = lax.dot_general(
        pick, of_mode, (((1,), (1,)), ((), ())), preferred_element_type=F32
    ).astype(BF16)
    row, col = iota((MIXED, DENSE), 0), iota((MIXED, DENSE), 1)
    part = over_pad(row)
    inner = row - part * PAD
    again = (col >= SLOTS).astype(jnp.int32) + (col >= 2 * SLOTS).astype(jnp.int32)
    dense = (col - again * SLOTS == part * QUOTA + inner) & (inner < QUOTA)
    dense = [(dense & (again < 2)).astype(BF16), (dense & (again == 2)).astype(BF16)]
    row, col = iota((SLOTS, DEPTH), 0), iota((SLOTS, DEPTH), 1)
    part = over_pad(col)
    inner = col - part * PAD
    rights = []
    for group in groups:
        pick = ((row == group * QUOTA + inner) & (inner < QUOTA)).astype(BF16)
        rights.append(dot(of_mode, pick).astype(BF16))
    term = over_pad(iota((MIXED, DEPTH), 1))
    totals = [[jnp.zeros((MIXED, DEPTH), F32)] * 2 for _ in groups]
    for k in range(TERMS):
        masked = coupling[k] * pattern[k].astype(F32)
        for level, part in enumerate(split(masked)):
            rows = dot(left, part).astype(BF16)
            for i, right in enumerate(rights):
                totals[i][level] = jnp.where(term == k, dot(rows, right), totals[i][level])
    for i in range(len(groups)):
        turned = jnp.zeros((DEPTH, DENSE), F32)
        for level in range(2):
            matrix = totals[i][level].astype(BF16)
            mixing[i, level * MIXED : (level + 1) * MIXED] = matrix
            turned = turned + lax.dot_general(
                matrix, dense[level], (((0,), (0,)), ((), ())), preferred_element_type=F32
            )
        turned_mixing[i] = turned.astype(BF16)


def mix(mixing, i, values):
    high, low = split(values)
    both = dot(mixing[i], high)
    return both[:MIXED] + both[MIXED:] + dot(mixing[i, :MIXED], low)


def slots_inside(block):
    zeros = jnp.zeros((PAD - QUOTA, ROWS, SIDE), F32)
    return jnp.swapaxes(jnp.concatenate([block, zeros], 0), 0, 1)


def kernel(
    u_hbm, mean_hbm, kl_hbm, pattern_hbm, coupling_hbm, slots_hbm, own_out, far_out,
    field, turned, coef, pattern, coupling, slots, mixing, turned_mixing, halo, edge, weight, centre, partial, near,
    gathered, dense, mixed_rows, blank,
    load_sem, store_sem, blank_sem,
    gather_send, gather_recv, share_send, share_recv,
    halo_send, halo_recv, edge_send, edge_recv, pass_send, pass_recv, near_send, near_recv, far_send, far_recv,
):
    place = lax.axis_index("space")
    mode = lax.axis_index("mode")
    planes = lax.axis_size("space")
    core = mode % 2
    sibling = mode + 1 - 2 * core
    across = (mode + 2) % 4
    diagonal = (sibling + 2) % 4
    along = place % RING
    mode_up = jnp.where(along == RING - 1, across, mode)
    mode_down = jnp.where(along == 0, across, mode)
    has_up = place < planes - 1
    has_down = place > 0
    up = (place + 1, mode_up)
    down = (place - 1, mode_down)
    level = mode // 2
    shared_in = along == 0
    shared_out = along == RING - 1
    sends = ((has_up, up), (has_down, down))
    comes = (has_down, has_up)

    loads = [
        pltpu.make_async_copy(u_hbm.at[:, 0], field, load_sem.at[0]),
        pltpu.make_async_copy(mean_hbm, coef.at[pl.ds(0, 1), pl.ds(ROWS, SIDE)], load_sem.at[1]),
        pltpu.make_async_copy(kl_hbm.at[:, 0], coef.at[pl.ds(1, TERMS - 1), pl.ds(ROWS, SIDE)], load_sem.at[2]),
        pltpu.make_async_copy(pattern_hbm, pattern, load_sem.at[3]),
        pltpu.make_async_copy(coupling_hbm, coupling, load_sem.at[4]),
        pltpu.make_async_copy(slots_hbm, slots, load_sem.at[5]),
    ]
    for i in (1, 2, 0, 3, 4, 5):
        loads[i].start()

    barrier = pltpu.get_barrier_semaphore()

    def greet(device):
        pl.semaphore_signal(barrier, inc=1, device_id=device, device_id_type=MESH)

    first_place, last_place = along == 0, along == RING - 1
    invites = has_down & first_place
    accepts = has_up & last_place
    pl.when(has_up & jnp.logical_not(last_place))(lambda: greet(up))
    pl.when(has_down & jnp.logical_not(first_place))(lambda: greet(down))
    greet((place, sibling))
    greet((place, across))

    zero_rows = jnp.zeros((TERMS, ROWS, SIDE), F32)
    coef[:, pl.ds(0, ROWS)] = zero_rows
    coef[:, pl.ds(ROWS + SIDE, ROWS)] = zero_rows
    turned[0] = jnp.zeros((PAD, SIDE), F32)
    turned[SIDE + 1] = jnp.zeros((PAD, SIDE), F32)

    for h in range(2):

        @pl.when(jnp.logical_not(comes[h]))
        def _():
            @pl.loop(0, CHUNKS)
            def _(j):
                halo[h, j] = jnp.zeros((QUOTA, ROWS, SIDE), F32)
                edge[h, j] = zero_rows

    loads[1].wait()
    loads[2].wait()
    count = 2 + has_up.astype(jnp.int32) + has_down.astype(jnp.int32) - invites.astype(jnp.int32)
    pl.semaphore_wait(barrier, count)
    pl.when(invites)(lambda: greet(down))
    pl.when(accepts)(lambda: greet(up))

    def rows_of(j):
        return pl.ds(pl.multiple_of(j * ROWS, ROWS), ROWS)

    def halo_copy(h, j):
        return pltpu.make_async_remote_copy(
            src_ref=u_hbm.at[:, 0, pl.ds(pl.multiple_of(j * ROWS, ROWS), ROWS)],
            dst_ref=halo.at[h, j],
            send_sem=halo_send.at[h, j],
            recv_sem=halo_recv.at[h, j],
            device_id=sends[h][1],
            device_id_type=MESH,
        )

    def edge_copy(h, p):
        j = 2 * p + core
        return pltpu.make_async_remote_copy(
            src_ref=coef.at[:, pl.ds(pl.multiple_of(ROWS + j * ROWS, ROWS), ROWS)],
            dst_ref=edge.at[h, j],
            send_sem=edge_send.at[h, p],
            recv_sem=edge_recv.at[h, p],
            device_id=sends[h][1],
            device_id_type=MESH,
        )

    def pass_copy(h, p, mine):
        j = 2 * p + (core if mine else 1 - core)
        return pltpu.make_async_remote_copy(
            src_ref=edge.at[h, j],
            dst_ref=edge.at[h, j],
            send_sem=pass_send.at[h, p],
            recv_sem=pass_recv.at[h, p],
            device_id=(place, sibling),
            device_id_type=MESH,
        )

    def share_copy(p):
        j = 2 * p + core
        return pltpu.make_async_remote_copy(
            src_ref=edge.at[0, j],
            dst_ref=edge.at[0, j],
            send_sem=share_send.at[p],
            recv_sem=share_recv.at[p],
            device_id=(place, across),
            device_id_type=MESH,
        )

    def near_copy(i, j):
        return pltpu.make_async_remote_copy(
            src_ref=partial.at[j, (sibling, diagonal)[i]],
            dst_ref=near.at[j, i],
            send_sem=near_send.at[i, j],
            recv_sem=near_recv.at[i, j],
            device_id=(place, sibling),
            device_id_type=MESH,
        )

    def far_copy(j):
        return pltpu.make_async_remote_copy(
            src_ref=partial.at[j, across],
            dst_ref=far_out.at[:, rows_of(j)],
            send_sem=far_send.at[j],
            recv_sem=far_recv.at[j],
            device_id=(place, across),
            device_id_type=MESH,
        )

    def own_copy(j):
        return pltpu.make_async_copy(partial.at[j, mode], own_out.at[:, rows_of(j)], store_sem.at[j])

    def send_edges(p, now):
        pl.when(now[0] & jnp.logical_not(shared_out))(lambda: edge_copy(0, p).start())
        pl.when(now[1])(lambda: edge_copy(1, p).start())

    def gather_copy(i, c):
        rows = pl.ds(pl.multiple_of((EARLY - 1 + c) * ROWS, ROWS), ROWS)
        group = (mode, mode, across)[i]
        return pltpu.make_async_remote_copy(
            src_ref=gathered.at[c, group] if i == 2 else u_hbm.at[:, 0, rows],
            dst_ref=gathered.at[c, group],
            send_sem=gather_send.at[i, c],
            recv_sem=gather_recv.at[i, c],
            device_id=(place, (across, sibling, sibling)[i]),
            device_id_type=MESH,
        )

    def late_copy(h, c):
        return pltpu.make_async_remote_copy(
            src_ref=partial.at[EARLY + c, h],
            dst_ref=halo.at[1, EARLY + c] if h == 1 else far_out.at[:, rows_of(EARLY + c)],
            send_sem=halo_send.at[h, EARLY + c],
            recv_sem=halo_recv.at[h, EARLY + c],
            device_id=sends[h][1],
            device_id_type=MESH,
        )

    goes = has_up & shared_out
    comes_shared = has_down & shared_in

    @pl.when(goes)
    def _():
        @pl.loop(0, PAIRS // 2)
        def _(q):
            edge_copy(0, 2 * q + mode_up // 2).start()

    def send_all(now):
        send_edges(0, now)

        @pl.loop(0, LOOPS)
        def _(p):
            pl.when(p < LOOPS - 1)(lambda: send_edges(p + 1, now))
            pl.when((p == 1) | (p == 2))(lambda: send_edges(LOOPS + p - 1, now))
            for j in (2 * p, 2 * p + 1):
                for h in range(2):
                    pl.when(now[h])(lambda h=h, j=j: halo_copy(h, j).start())

    send_all((has_up, has_down & jnp.logical_not(first_place)))

    @pl.loop(0, GATHERED)
    def _(c):
        gather_copy(0, c).start()
        gather_copy(1, c).start()

    blank_copy = pltpu.make_async_copy(blank, far_out.at[:, pl.ds(EARLY * ROWS, LATE * ROWS)], blank_sem)

    @pl.when(jnp.logical_not(has_down))
    def _():
        blank[...] = jnp.zeros_like(blank)
        blank_copy.start()

    dense[GATHERED * ROWS] = jnp.zeros((DENSE, SIDE), BF16)

    loads[3].wait()
    loads[4].wait()
    loads[5].wait()
    build_mixing((mode, mode_down, mode_up), pattern, coupling, slots, mixing, turned_mixing)
    loads[0].wait()

    @pl.loop(0, CHUNKS)
    def _(j):
        turned[pl.ds(j * ROWS + 1, ROWS)] = slots_inside(field[:, rows_of(j)])

    @pl.when(invites)
    def _():
        pl.semaphore_wait(barrier, 1)
        send_all((place < 0, has_down))

    def relay_edges(p):
        for h in range(2):

            @pl.when(comes[h])
            def _():
                if h == 0:
                    pl.when(jnp.logical_not(shared_in))(lambda: edge_copy(0, p).wait_recv())
                    pl.when(shared_in & (p % 2 != level))(lambda: share_copy(p).wait_recv())
                else:
                    edge_copy(1, p).wait_recv()
                pass_copy(h, p, True).start()

    def take_edges(p):
        for h in range(2):
            pl.when(comes[h])(lambda h=h: pass_copy(h, p, False).wait_recv())

    first = iota((1, 1, SIDE), 2) == 0
    last = iota((1, 1, SIDE), 2) == SIDE - 1

    def set_weights(slot, j):
        block = coef[:, pl.ds(pl.multiple_of(j * ROWS, ROWS), 3 * ROWS)]
        here = block[:, ROWS : 2 * ROWS]
        right = 0.5 * (here + jnp.where(last, 0.0, pltpu.roll(here, SIDE - 1, 2)))
        left = 0.5 * (here + jnp.where(first, 0.0, pltpu.roll(here, 1, 2)))
        after = 0.5 * (here + block[:, ROWS + 1 : 2 * ROWS + 1])
        before = 0.5 * (here + block[:, ROWS - 1 : 2 * ROWS - 1])
        below = 0.5 * (here + edge[0, j])
        above = 0.5 * (here + edge[1, j])
        weight[slot, 0] = right + left + after + before + below + above
        weight[slot, 1] = jnp.where(last, 0.0, -right)
        weight[slot, 2] = jnp.where(first, 0.0, -left)
        weight[slot, 3] = -after
        weight[slot, 4] = -before
        weight[slot, 5] = -below
        weight[slot, 6] = -above

    def own_part(j):
        set_weights(0, j)
        for r in range(0, ROWS, 2):
            sides = []
            for q in (r, r + 1):
                y = j * ROWS + q + 1
                own = turned[y]
                values = (own, pltpu.roll(own, SIDE - 1, 1), pltpu.roll(own, 1, 1), turned[y + 1], turned[y - 1])
                terms = []
                for k in range(TERMS):
                    total = weight[0, 0, k, q : q + 1] * values[0]
                    for i in range(1, 5):
                        total = total + weight[0, i, k, q : q + 1] * values[i]
                    terms.append(total)
                sides.append(jnp.concatenate(terms + [jnp.zeros((DEPTH - TERMS * PAD, SIDE), F32)], 0))
            mixed = mix(mixing, 0, jnp.concatenate(sides, 1))
            centre[r] = mixed[:, :SIDE]
            centre[r + 1] = mixed[:, SIDE:]

    def halo_part(j):
        for h in range(2):
            pl.when(comes[h])(lambda h=h: halo_copy(h, j).wait_recv())
        beside = [slots_inside(halo[h, j]) for h in range(2)]
        results = []
        for r in range(0, ROWS, 2):
            mixed = jnp.concatenate([centre[r], centre[r + 1]], 1)
            for h in range(2):
                sides = []
                for q in (r, r + 1):
                    terms = [weight[0, 5 + h, k, q : q + 1] * beside[h][q] for k in range(TERMS)]
                    sides.append(jnp.concatenate(terms + [jnp.zeros((DEPTH - TERMS * PAD, SIDE), F32)], 0))
                mixed = mixed + mix(mixing, 1 + h, jnp.concatenate(sides, 1))
            results.extend([mixed[None, :, :SIDE], mixed[None, :, SIDE:]])
        by_slot = jnp.swapaxes(jnp.concatenate(results, 0), 0, 1)
        for g in range(GROUPS):
            partial[j, g] = by_slot[g * PAD : g * PAD + QUOTA]
        near_copy(1, j).start()
        near_copy(0, j).start()

    def join(j):
        near_copy(1, j).wait_recv()
        partial[j, across] = partial[j, across] + near[j, 1]
        far_copy(j).start()
        near_copy(0, j).wait_recv()
        partial[j, mode] = partial[j, mode] + near[j, 0]
        own_copy(j).start()

    at_end = (along == 0) | (along == RING - 1)
    other = jnp.where(along == 0, 1, 2)
    used = (jnp.where(along == RING - 1, 1, 0), jnp.where(along == 0, 1, 0))

    def pass_gathered(c):
        gather_copy(0, c).wait_recv()
        gather_copy(2, c).start()

    def turn_gathered(c):
        gather_copy(1, c).wait_recv()
        gather_copy(2, c).wait_recv()
        rows = pl.ds(pl.multiple_of((EARLY - 1 + c) * ROWS, ROWS), ROWS)
        gathered[c, mode] = field[:, rows]
        block = gathered[c].reshape(SLOTS, ROWS, SIDE)
        high = block.astype(BF16).astype(F32)
        zeros = jnp.zeros((DENSE - 3 * SLOTS, ROWS, SIDE), F32)
        block = jnp.concatenate([high, block - high, high, zeros], 0)
        dense[pl.ds(c * ROWS, ROWS)] = jnp.swapaxes(block, 0, 1).astype(BF16)

    def mix_rows(slot, i, c):
        for r in range(0, ROWS + 2, 2):
            y = c * ROWS + ROWS - 1 + r
            mixed = dot(turned_mixing[i], jnp.concatenate([dense[y], dense[y + 1]], 1))
            mixed_rows[slot, r] = mixed[:, :SIDE]
            mixed_rows[slot, r + 1] = mixed[:, SIDE:]

    def by_slot(rows):
        return jnp.swapaxes(jnp.concatenate([row[None] for row in rows], 0), 0, 1)[:QUOTA]

    def late_part(c):
        set_weights(1, EARLY + c)
        mix_rows(0, 0, c)
        pl.when(at_end)(lambda: mix_rows(1, other, c))

        def term(slot, r, k):
            return mixed_rows[slot, r + 1, k * PAD : (k + 1) * PAD]

        for h in range(2):
            rows = []
            for r in range(ROWS):
                total = weight[1, 6 - h, 0, r : r + 1] * term(used[h], r, 0)
                for k in range(1, TERMS):
                    total = total + weight[1, 6 - h, k, r : r + 1] * term(used[h], r, k)
                rows.append(total)
            partial[EARLY + c, h] = by_slot(rows)
            pl.when(sends[h][0])(lambda h=h: late_copy(h, c).start())
        rows = []
        for r in range(ROWS):
            total = jnp.zeros((PAD, SIDE), F32)
            for k in range(TERMS):
                own = term(0, r, k)
                values = (own, pltpu.roll(own, SIDE - 1, 1), pltpu.roll(own, 1, 1), term(0, r + 1, k), term(0, r - 1, k))
                for i in range(5):
                    total = total + weight[1, i, k, r : r + 1] * values[i]
            rows.append(total)
        partial[EARLY + c, 2] = by_slot(rows)

    def late_join(c):
        j = EARLY + c
        pl.when(has_up)(lambda: late_copy(1, c).wait_recv())
        partial[j, 2] = partial[j, 2] + halo[1, j]
        late_store(c).start()

    def late_store(c):
        j = EARLY + c
        return pltpu.make_async_copy(partial.at[j, 2], own_out.at[:, rows_of(j)], store_sem.at[j])

    @pl.when(comes_shared)
    def _():
        @pl.loop(0, PAIRS // 2)
        def _(q):
            edge_copy(0, 2 * q + level).wait_recv()
            share_copy(2 * q + level).start()

    relay_edges(0)
    take_edges(0)
    own_part(0)

    @pl.loop(0, LOOPS)
    def _(p):
        extra = (p == 1) | (p == 2)
        late = (p == 2) | (p == 3)
        halo_part(2 * p)
        pl.when(p > 0)(lambda: join(2 * p - 1))
        pl.when(p < LOOPS - 1)(lambda: relay_edges(p + 1))
        pl.when(extra)(lambda: relay_edges(LOOPS + p - 1))
        own_part(2 * p + 1)
        pl.when(late)(lambda: late_part(2 * p - 4))

        @pl.when(p == 0)
        def _():
            pass_gathered(0)
            pass_gathered(1)

        @pl.when(p == 1)
        def _():
            pass_gathered(3)

        halo_part(2 * p + 1)
        join(2 * p)

        @pl.when(p < LOOPS - 1)
        def _():
            take_edges(p + 1)
            own_part(2 * p + 2)

        pl.when(extra)(lambda: take_edges(LOOPS + p - 1))
        pl.when(late)(lambda: late_part(2 * p - 3))
        pl.when(p == 0)(lambda: pass_gathered(2))

        @pl.when(p == 1)
        def _():
            pass_gathered(4)
            pl.loop(0, GATHERED)(turn_gathered)


    join(EARLY - 1)

    @pl.loop(0, PAIRS)
    def _(p):
        for h in range(2):
            pl.when(comes[h])(lambda h=h: pass_copy(h, p, True).wait_send())

        pl.when(has_up & (jnp.logical_not(shared_out) | (p % 2 == mode_up // 2)))(lambda: edge_copy(0, p).wait_send())
        pl.when(has_down)(lambda: edge_copy(1, p).wait_send())
        pl.when(comes_shared & (p % 2 == level))(lambda: share_copy(p).wait_send())

    @pl.loop(0, GATHERED)
    def _(c):
        for i in range(3):
            gather_copy(i, c).wait_send()

    @pl.loop(0, EARLY)
    def _(j):
        for h in range(2):
            pl.when(sends[h][0])(lambda h=h: halo_copy(h, j).wait_send())
        for i in range(2):
            near_copy(i, j).wait_send()

    pl.when(jnp.logical_not(has_down))(blank_copy.wait)

    pl.loop(0, LATE)(late_join)

    @pl.loop(0, EARLY)
    def _(j):
        own_copy(j).wait()
        far_copy(j).wait()

    @pl.loop(0, LATE)
    def _(c):
        for h in range(2):
            pl.when(sends[h][0])(lambda h=h: late_copy(h, c).wait_send())
        late_store(c).wait()
        pl.when(has_down)(lambda: late_copy(0, c).wait_recv())


def on_device(chaos_field, mean_field, kl_fields, pattern, coupling, slot_mode):
    dma = pltpu.SemaphoreType.DMA
    result = pltpu.VMEM((QUOTA, SIDE, SIDE), F32)
    operands = (chaos_field, mean_field, kl_fields, pattern, coupling, slot_mode.reshape(1, SLOTS))
    operands = [pltpu.with_memory_space_constraint(operand, pltpu.HBM) for operand in operands]
    own, far = pl.pallas_call(
        kernel,
        out_shape=(result, result),
        in_specs=[pl.BlockSpec(memory_space=pltpu.HBM)] * len(operands),
        out_specs=(pl.BlockSpec(memory_space=pl.ANY),) * 2,
        scratch_shapes=[
            pltpu.VMEM((QUOTA, SIDE, SIDE), F32),
            pltpu.VMEM((SIDE + 2, PAD, SIDE), F32),
            pltpu.VMEM((TERMS, SIDE + 2 * ROWS, SIDE), F32),
            pltpu.VMEM((TERMS, SLOTS, SLOTS), jnp.int32),
            pltpu.VMEM((TERMS, SLOTS, SLOTS), F32),
            pltpu.VMEM((1, SLOTS), jnp.int32),
            pltpu.VMEM((3, 2 * MIXED, DEPTH), BF16),
            pltpu.VMEM((3, DEPTH, DENSE), BF16),
            pltpu.VMEM((2, CHUNKS, QUOTA, ROWS, SIDE), F32),
            pltpu.VMEM((2, CHUNKS, TERMS, ROWS, SIDE), F32),
            pltpu.VMEM((2, 7, TERMS, ROWS, SIDE), F32),
            pltpu.VMEM((ROWS, MIXED, SIDE), F32),
            pltpu.VMEM((CHUNKS, GROUPS, QUOTA, ROWS, SIDE), F32),
            pltpu.VMEM((EARLY, 2, QUOTA, ROWS, SIDE), F32),
            pltpu.VMEM((GATHERED, GROUPS, QUOTA, ROWS, SIDE), F32),
            pltpu.VMEM((GATHERED * ROWS + 1, DENSE, SIDE), BF16),
            pltpu.VMEM((2, ROWS + 2, DEPTH, SIDE), F32),
            pltpu.VMEM((QUOTA, LATE * ROWS, SIDE), F32),
            dma((6,)),
            dma((CHUNKS,)),
            dma,
            dma((3, GATHERED)),
            dma((3, GATHERED)),
            dma((PAIRS,)),
            dma((PAIRS,)),
            dma((2, CHUNKS)),
            dma((2, CHUNKS)),
            dma((2, PAIRS)),
            dma((2, PAIRS)),
            dma((2, PAIRS)),
            dma((2, PAIRS)),
            dma((2, CHUNKS)),
            dma((2, CHUNKS)),
            dma((CHUNKS,)),
            dma((CHUNKS,)),
        ],
        compiler_params=pltpu.CompilerParams(
            collective_id=0, has_side_effects=True, vmem_limit_bytes=48 << 20
        ),
    )(*operands)
    return (own + far).reshape(QUOTA, 1, SIDE, SIDE)


def solution(mesh):
    in_specs = (
        P("mode", "space", None, None),
        P("space", None, None),
        P(None, "space", None, None),
        P(),
        P(),
        P(),
    )
    out_specs = P("mode", "space", None, None)
    return jax.shard_map(
        on_device, mesh=mesh, in_specs=in_specs, out_specs=out_specs, check_vma=False
    )
```

```python
import jax
import jax.numpy as jnp
from jax import lax
from jax.experimental import pallas as pl
from jax.experimental.pallas import tpu as pltpu
from jax.sharding import PartitionSpec as P

MESH = pl.DeviceIdType.MESH
RING = 8
GROUPS = 4
QUOTA = 21
SLOTS = GROUPS * QUOTA
TERMS = 7
ROWS = 8
PAD = 24
DEPTH = 176
SIDE = 128
CHUNKS = SIDE // ROWS
PAIRS = CHUNKS // 2
LATE = 4
EARLY = CHUNKS - LATE
LOOPS = EARLY // 2
GATHERED = LATE + 1
DENSE = 256
MIXED = GROUPS * PAD
F32 = jnp.float32
BF16 = jnp.bfloat16


def split(value):
    high = value.astype(BF16)
    return high, (value - high.astype(F32)).astype(BF16)


def dot(left, right):
    return jnp.dot(left, right, preferred_element_type=F32)


def iota(shape, dim):
    return lax.broadcasted_iota(jnp.int32, shape, dim)


def over_pad(index):
    return (index * 43691) >> 20


def build_mixing(groups, pattern, coupling, slots, mixing, turned_mixing):
    of_mode = (iota((SLOTS, SLOTS), 0) == slots[...]).astype(BF16)
    row, col = iota((MIXED, SLOTS), 0), iota((MIXED, SLOTS), 1)
    part = over_pad(row)
    inner = row - part * PAD
    pick = ((col == part * QUOTA + inner) & (inner < QUOTA)).astype(BF16)
    left = lax.dot_general(
        pick, of_mode, (((1,), (1,)), ((), ())), preferred_element_type=F32
    ).astype(BF16)
    row, col = iota((MIXED, DENSE), 0), iota((MIXED, DENSE), 1)
    part = over_pad(row)
    inner = row - part * PAD
    again = (col >= SLOTS).astype(jnp.int32) + (col >= 2 * SLOTS).astype(jnp.int32)
    dense = (col - again * SLOTS == part * QUOTA + inner) & (inner < QUOTA)
    dense = [(dense & (again < 2)).astype(BF16), (dense & (again == 2)).astype(BF16)]
    row, col = iota((SLOTS, DEPTH), 0), iota((SLOTS, DEPTH), 1)
    part = over_pad(col)
    inner = col - part * PAD
    rights = []
    for group in groups:
        pick = ((row == group * QUOTA + inner) & (inner < QUOTA)).astype(BF16)
        rights.append(dot(of_mode, pick).astype(BF16))
    term = over_pad(iota((MIXED, DEPTH), 1))
    totals = [[jnp.zeros((MIXED, DEPTH), F32)] * 2 for _ in groups]
    for k in range(TERMS):
        masked = coupling[k] * pattern[k].astype(F32)
        for level, part in enumerate(split(masked)):
            rows = dot(left, part).astype(BF16)
            for i, right in enumerate(rights):
                totals[i][level] = jnp.where(term == k, dot(rows, right), totals[i][level])
    for i in range(len(groups)):
        turned = jnp.zeros((DEPTH, DENSE), F32)
        for level in range(2):
            matrix = totals[i][level].astype(BF16)
            mixing[i, level * MIXED : (level + 1) * MIXED] = matrix
            turned = turned + lax.dot_general(
                matrix, dense[level], (((0,), (0,)), ((), ())), preferred_element_type=F32
            )
        turned_mixing[i] = turned.astype(BF16)


def mix(mixing, i, values):
    high, low = split(values)
    both = dot(mixing[i], high)
    return both[:MIXED] + both[MIXED:] + dot(mixing[i, :MIXED], low)


def slots_inside(block):
    zeros = jnp.zeros((PAD - QUOTA, ROWS, SIDE), F32)
    return jnp.swapaxes(jnp.concatenate([block, zeros], 0), 0, 1)


def kernel(
    u_hbm, mean_hbm, kl_hbm, pattern_hbm, coupling_hbm, slots_hbm, own_out, far_out,
    field, turned, coef, pattern, coupling, slots, mixing, turned_mixing, halo, edge, weight, centre, partial, near,
    gathered, dense, mixed_rows, blank,
    load_sem, store_sem, blank_sem,
    gather_send, gather_recv, share_send, share_recv,
    halo_send, halo_recv, edge_send, edge_recv, pass_send, pass_recv, near_send, near_recv, far_send, far_recv,
):
    place = lax.axis_index("space")
    mode = lax.axis_index("mode")
    planes = lax.axis_size("space")
    core = mode % 2
    sibling = mode + 1 - 2 * core
    across = (mode + 2) % 4
    diagonal = (sibling + 2) % 4
    along = place % RING
    mode_up = jnp.where(along == RING - 1, across, mode)
    mode_down = jnp.where(along == 0, across, mode)
    has_up = place < planes - 1
    has_down = place > 0
    up = (place + 1, mode_up)
    down = (place - 1, mode_down)
    level = mode // 2
    shared_in = along == 0
    shared_out = along == RING - 1
    sends = ((has_up, up), (has_down, down))
    comes = (has_down, has_up)

    loads = [
        pltpu.make_async_copy(u_hbm.at[:, 0], field, load_sem.at[0]),
        pltpu.make_async_copy(mean_hbm, coef.at[pl.ds(0, 1), pl.ds(ROWS, SIDE)], load_sem.at[1]),
        pltpu.make_async_copy(kl_hbm.at[:, 0], coef.at[pl.ds(1, TERMS - 1), pl.ds(ROWS, SIDE)], load_sem.at[2]),
        pltpu.make_async_copy(pattern_hbm, pattern, load_sem.at[3]),
        pltpu.make_async_copy(coupling_hbm, coupling, load_sem.at[4]),
        pltpu.make_async_copy(slots_hbm, slots, load_sem.at[5]),
    ]
    for i in (1, 2, 0, 3, 4, 5):
        loads[i].start()

    barrier = pltpu.get_barrier_semaphore()

    def greet(device):
        pl.semaphore_signal(barrier, inc=1, device_id=device, device_id_type=MESH)

    first_place, last_place = along == 0, along == RING - 1
    invites = has_down & first_place
    accepts = has_up & last_place
    pl.when(has_up & jnp.logical_not(last_place))(lambda: greet(up))
    pl.when(has_down & jnp.logical_not(first_place))(lambda: greet(down))
    greet((place, sibling))
    greet((place, across))

    zero_rows = jnp.zeros((TERMS, ROWS, SIDE), F32)
    coef[:, pl.ds(0, ROWS)] = zero_rows
    coef[:, pl.ds(ROWS + SIDE, ROWS)] = zero_rows
    turned[0] = jnp.zeros((PAD, SIDE), F32)
    turned[SIDE + 1] = jnp.zeros((PAD, SIDE), F32)

    for h in range(2):

        @pl.when(jnp.logical_not(comes[h]))
        def _():
            @pl.loop(0, CHUNKS)
            def _(j):
                halo[h, j] = jnp.zeros((QUOTA, ROWS, SIDE), F32)
                edge[h, j] = zero_rows

    count = 2 + has_up.astype(jnp.int32) + has_down.astype(jnp.int32) - invites.astype(jnp.int32)
    pl.semaphore_wait(barrier, count)
    pl.when(invites)(lambda: greet(down))
    pl.when(accepts)(lambda: greet(up))

    def rows_of(j):
        return pl.ds(pl.multiple_of(j * ROWS, ROWS), ROWS)

    def halo_copy(h, j):
        return pltpu.make_async_remote_copy(
            src_ref=u_hbm.at[:, 0, pl.ds(pl.multiple_of(j * ROWS, ROWS), ROWS)],
            dst_ref=halo.at[h, j],
            send_sem=halo_send.at[h, j],
            recv_sem=halo_recv.at[h, j],
            device_id=sends[h][1],
            device_id_type=MESH,
        )

    def edge_copy(h, p):
        j = 2 * p + core
        return pltpu.make_async_remote_copy(
            src_ref=coef.at[:, pl.ds(pl.multiple_of(ROWS + j * ROWS, ROWS), ROWS)],
            dst_ref=edge.at[h, j],
            send_sem=edge_send.at[h, p],
            recv_sem=edge_recv.at[h, p],
            device_id=sends[h][1],
            device_id_type=MESH,
        )

    def pass_copy(h, p, mine):
        j = 2 * p + (core if mine else 1 - core)
        return pltpu.make_async_remote_copy(
            src_ref=edge.at[h, j],
            dst_ref=edge.at[h, j],
            send_sem=pass_send.at[h, p],
            recv_sem=pass_recv.at[h, p],
            device_id=(place, sibling),
            device_id_type=MESH,
        )

    def share_copy(p):
        j = 2 * p + core
        return pltpu.make_async_remote_copy(
            src_ref=edge.at[0, j],
            dst_ref=edge.at[0, j],
            send_sem=share_send.at[p],
            recv_sem=share_recv.at[p],
            device_id=(place, across),
            device_id_type=MESH,
        )

    def near_copy(i, j):
        return pltpu.make_async_remote_copy(
            src_ref=partial.at[j, (sibling, diagonal)[i]],
            dst_ref=near.at[j, i],
            send_sem=near_send.at[i, j],
            recv_sem=near_recv.at[i, j],
            device_id=(place, sibling),
            device_id_type=MESH,
        )

    def far_copy(j):
        return pltpu.make_async_remote_copy(
            src_ref=partial.at[j, across],
            dst_ref=far_out.at[:, rows_of(j)],
            send_sem=far_send.at[j],
            recv_sem=far_recv.at[j],
            device_id=(place, across),
            device_id_type=MESH,
        )

    def own_copy(j):
        return pltpu.make_async_copy(partial.at[j, mode], own_out.at[:, rows_of(j)], store_sem.at[j])

    def send_edges(p, now):
        pl.when(now[0] & jnp.logical_not(shared_out))(lambda: edge_copy(0, p).start())
        pl.when(now[1])(lambda: edge_copy(1, p).start())

    def gather_copy(i, c):
        rows = pl.ds(pl.multiple_of((EARLY - 1 + c) * ROWS, ROWS), ROWS)
        group = (mode, mode, across)[i]
        return pltpu.make_async_remote_copy(
            src_ref=gathered.at[c, group] if i == 2 else u_hbm.at[:, 0, rows],
            dst_ref=gathered.at[c, group],
            send_sem=gather_send.at[i, c],
            recv_sem=gather_recv.at[i, c],
            device_id=(place, (across, sibling, sibling)[i]),
            device_id_type=MESH,
        )

    def late_copy(h, c):
        return pltpu.make_async_remote_copy(
            src_ref=partial.at[EARLY + c, h],
            dst_ref=halo.at[1, EARLY + c] if h == 1 else far_out.at[:, rows_of(EARLY + c)],
            send_sem=halo_send.at[h, EARLY + c],
            recv_sem=halo_recv.at[h, EARLY + c],
            device_id=sends[h][1],
            device_id_type=MESH,
        )

    first_now = (has_up, has_down & jnp.logical_not(first_place))
    for h in range(2):
        pl.when(first_now[h])(lambda h=h: halo_copy(h, 0).start())
    loads[1].wait()
    loads[2].wait()
    goes = has_up & shared_out
    comes_shared = has_down & shared_in

    @pl.when(goes)
    def _():
        @pl.loop(0, PAIRS // 2)
        def _(q):
            edge_copy(0, 2 * q + mode_up // 2).start()

    def send_all(now, start):
        send_edges(0, now)

        @pl.loop(0, LOOPS)
        def _(p):
            pl.when(p < LOOPS - 1)(lambda: send_edges(p + 1, now))
            pl.when((p == 1) | (p == 2))(lambda: send_edges(LOOPS + p - 1, now))
            for j in (2 * p, 2 * p + 1):
                for h in range(2):
                    pl.when(now[h] & (j >= start))(lambda h=h, j=j: halo_copy(h, j).start())

    send_all(first_now, 1)

    @pl.loop(0, GATHERED)
    def _(c):
        gather_copy(0, c).start()
        gather_copy(1, c).start()

    blank_copy = pltpu.make_async_copy(blank, far_out.at[:, pl.ds(EARLY * ROWS, LATE * ROWS)], blank_sem)

    @pl.when(jnp.logical_not(has_down))
    def _():
        blank[...] = jnp.zeros_like(blank)
        blank_copy.start()

    dense[GATHERED * ROWS] = jnp.zeros((DENSE, SIDE), BF16)

    loads[3].wait()
    loads[4].wait()
    loads[5].wait()
    build_mixing((mode, mode_down, mode_up), pattern, coupling, slots, mixing, turned_mixing)
    loads[0].wait()

    @pl.loop(0, CHUNKS)
    def _(j):
        turned[pl.ds(j * ROWS + 1, ROWS)] = slots_inside(field[:, rows_of(j)])

    @pl.when(invites)
    def _():
        pl.semaphore_wait(barrier, 1)
        send_all((place < 0, has_down), 0)

    def relay_edges(p):
        for h in range(2):

            @pl.when(comes[h])
            def _():
                if h == 0:
                    pl.when(jnp.logical_not(shared_in))(lambda: edge_copy(0, p).wait_recv())
                    pl.when(shared_in & (p % 2 != level))(lambda: share_copy(p).wait_recv())
                else:
                    edge_copy(1, p).wait_recv()
                pass_copy(h, p, True).start()

    def take_edges(p):
        for h in range(2):
            pl.when(comes[h])(lambda h=h: pass_copy(h, p, False).wait_recv())

    first = iota((1, 1, SIDE), 2) == 0
    last = iota((1, 1, SIDE), 2) == SIDE - 1

    def set_weights(slot, j):
        block = coef[:, pl.ds(pl.multiple_of(j * ROWS, ROWS), 3 * ROWS)]
        here = block[:, ROWS : 2 * ROWS]
        right = 0.5 * (here + jnp.where(last, 0.0, pltpu.roll(here, SIDE - 1, 2)))
        left = 0.5 * (here + jnp.where(first, 0.0, pltpu.roll(here, 1, 2)))
        after = 0.5 * (here + block[:, ROWS + 1 : 2 * ROWS + 1])
        before = 0.5 * (here + block[:, ROWS - 1 : 2 * ROWS - 1])
        below = 0.5 * (here + edge[0, j])
        above = 0.5 * (here + edge[1, j])
        weight[slot, 0] = right + left + after + before + below + above
        weight[slot, 1] = jnp.where(last, 0.0, -right)
        weight[slot, 2] = jnp.where(first, 0.0, -left)
        weight[slot, 3] = -after
        weight[slot, 4] = -before
        weight[slot, 5] = -below
        weight[slot, 6] = -above

    def own_part(j):
        set_weights(0, j)
        for r in range(0, ROWS, 2):
            sides = []
            for q in (r, r + 1):
                y = j * ROWS + q + 1
                own = turned[y]
                values = (own, pltpu.roll(own, SIDE - 1, 1), pltpu.roll(own, 1, 1), turned[y + 1], turned[y - 1])
                terms = []
                for k in range(TERMS):
                    total = weight[0, 0, k, q : q + 1] * values[0]
                    for i in range(1, 5):
                        total = total + weight[0, i, k, q : q + 1] * values[i]
                    terms.append(total)
                sides.append(jnp.concatenate(terms + [jnp.zeros((DEPTH - TERMS * PAD, SIDE), F32)], 0))
            mixed = mix(mixing, 0, jnp.concatenate(sides, 1))
            centre[r] = mixed[:, :SIDE]
            centre[r + 1] = mixed[:, SIDE:]

    def halo_part(j):
        for h in range(2):
            pl.when(comes[h])(lambda h=h: halo_copy(h, j).wait_recv())
        beside = [slots_inside(halo[h, j]) for h in range(2)]
        results = []
        for r in range(0, ROWS, 2):
            mixed = jnp.concatenate([centre[r], centre[r + 1]], 1)
            for h in range(2):
                sides = []
                for q in (r, r + 1):
                    terms = [weight[0, 5 + h, k, q : q + 1] * beside[h][q] for k in range(TERMS)]
                    sides.append(jnp.concatenate(terms + [jnp.zeros((DEPTH - TERMS * PAD, SIDE), F32)], 0))
                mixed = mixed + mix(mixing, 1 + h, jnp.concatenate(sides, 1))
            results.extend([mixed[None, :, :SIDE], mixed[None, :, SIDE:]])
        by_slot = jnp.swapaxes(jnp.concatenate(results, 0), 0, 1)
        for g in range(GROUPS):
            partial[j, g] = by_slot[g * PAD : g * PAD + QUOTA]
        near_copy(1, j).start()
        near_copy(0, j).start()

    def join(j):
        near_copy(1, j).wait_recv()
        partial[j, across] = partial[j, across] + near[j, 1]
        far_copy(j).start()
        near_copy(0, j).wait_recv()
        partial[j, mode] = partial[j, mode] + near[j, 0]
        own_copy(j).start()

    at_end = (along == 0) | (along == RING - 1)
    other = jnp.where(along == 0, 1, 2)
    used = (jnp.where(along == RING - 1, 1, 0), jnp.where(along == 0, 1, 0))

    def pass_gathered(c):
        gather_copy(0, c).wait_recv()
        gather_copy(2, c).start()

    def turn_gathered(c):
        gather_copy(1, c).wait_recv()
        gather_copy(2, c).wait_recv()
        rows = pl.ds(pl.multiple_of((EARLY - 1 + c) * ROWS, ROWS), ROWS)
        gathered[c, mode] = field[:, rows]
        block = gathered[c].reshape(SLOTS, ROWS, SIDE)
        high = block.astype(BF16).astype(F32)
        zeros = jnp.zeros((DENSE - 3 * SLOTS, ROWS, SIDE), F32)
        block = jnp.concatenate([high, block - high, high, zeros], 0)
        dense[pl.ds(c * ROWS, ROWS)] = jnp.swapaxes(block, 0, 1).astype(BF16)

    def mix_rows(slot, i, c):
        for r in range(0, ROWS + 2, 2):
            y = c * ROWS + ROWS - 1 + r
            mixed = dot(turned_mixing[i], jnp.concatenate([dense[y], dense[y + 1]], 1))
            mixed_rows[slot, r] = mixed[:, :SIDE]
            mixed_rows[slot, r + 1] = mixed[:, SIDE:]

    def by_slot(rows):
        return jnp.swapaxes(jnp.concatenate([row[None] for row in rows], 0), 0, 1)[:QUOTA]

    def late_part(c):
        set_weights(1, EARLY + c)
        mix_rows(0, 0, c)
        pl.when(at_end)(lambda: mix_rows(1, other, c))

        def term(slot, r, k):
            return mixed_rows[slot, r + 1, k * PAD : (k + 1) * PAD]

        for h in range(2):
            rows = []
            for r in range(ROWS):
                total = weight[1, 6 - h, 0, r : r + 1] * term(used[h], r, 0)
                for k in range(1, TERMS):
                    total = total + weight[1, 6 - h, k, r : r + 1] * term(used[h], r, k)
                rows.append(total)
            partial[EARLY + c, h] = by_slot(rows)
            pl.when(sends[h][0])(lambda h=h: late_copy(h, c).start())
        rows = []
        for r in range(ROWS):
            total = jnp.zeros((PAD, SIDE), F32)
            for k in range(TERMS):
                own = term(0, r, k)
                values = (own, pltpu.roll(own, SIDE - 1, 1), pltpu.roll(own, 1, 1), term(0, r + 1, k), term(0, r - 1, k))
                for i in range(5):
                    total = total + weight[1, i, k, r : r + 1] * values[i]
            rows.append(total)
        partial[EARLY + c, 2] = by_slot(rows)

    def late_join(c):
        j = EARLY + c
        pl.when(has_up)(lambda: late_copy(1, c).wait_recv())
        partial[j, 2] = partial[j, 2] + halo[1, j]
        late_store(c).start()

    def late_store(c):
        j = EARLY + c
        return pltpu.make_async_copy(partial.at[j, 2], own_out.at[:, rows_of(j)], store_sem.at[j])

    def share(q):
        edge_copy(0, 2 * q + level).wait_recv()
        share_copy(2 * q + level).start()

    @pl.when(comes_shared)
    def _():
        share(0)

    relay_edges(0)
    take_edges(0)
    own_part(0)

    @pl.when(comes_shared)
    def _():
        pl.loop(1, PAIRS // 2)(share)

    @pl.loop(0, LOOPS)
    def _(p):
        extra = (p == 1) | (p == 2)
        late = (p == 2) | (p == 3)
        halo_part(2 * p)
        pl.when(p > 0)(lambda: join(2 * p - 1))
        pl.when(p < LOOPS - 1)(lambda: relay_edges(p + 1))
        pl.when(extra)(lambda: relay_edges(LOOPS + p - 1))
        own_part(2 * p + 1)
        pl.when(late)(lambda: late_part(2 * p - 4))

        @pl.when(p == 0)
        def _():
            pass_gathered(0)
            pass_gathered(1)

        @pl.when(p == 1)
        def _():
            pass_gathered(3)

        halo_part(2 * p + 1)
        join(2 * p)

        @pl.when(p < LOOPS - 1)
        def _():
            take_edges(p + 1)
            own_part(2 * p + 2)

        pl.when(extra)(lambda: take_edges(LOOPS + p - 1))
        pl.when(late)(lambda: late_part(2 * p - 3))
        pl.when(p == 0)(lambda: pass_gathered(2))

        @pl.when(p == 1)
        def _():
            pass_gathered(4)
            pl.loop(0, GATHERED)(turn_gathered)


    join(EARLY - 1)

    @pl.loop(0, PAIRS)
    def _(p):
        for h in range(2):
            pl.when(comes[h])(lambda h=h: pass_copy(h, p, True).wait_send())

        pl.when(has_up & (jnp.logical_not(shared_out) | (p % 2 == mode_up // 2)))(lambda: edge_copy(0, p).wait_send())
        pl.when(has_down)(lambda: edge_copy(1, p).wait_send())
        pl.when(comes_shared & (p % 2 == level))(lambda: share_copy(p).wait_send())

    @pl.loop(0, GATHERED)
    def _(c):
        for i in range(3):
            gather_copy(i, c).wait_send()

    @pl.loop(0, EARLY)
    def _(j):
        for h in range(2):
            pl.when(sends[h][0])(lambda h=h: halo_copy(h, j).wait_send())
        for i in range(2):
            near_copy(i, j).wait_send()

    pl.when(jnp.logical_not(has_down))(blank_copy.wait)

    pl.loop(0, LATE)(late_join)

    @pl.loop(0, EARLY)
    def _(j):
        own_copy(j).wait()
        far_copy(j).wait()

    @pl.loop(0, LATE)
    def _(c):
        for h in range(2):
            pl.when(sends[h][0])(lambda h=h: late_copy(h, c).wait_send())
        late_store(c).wait()
        pl.when(has_down)(lambda: late_copy(0, c).wait_recv())


def on_device(chaos_field, mean_field, kl_fields, pattern, coupling, slot_mode):
    dma = pltpu.SemaphoreType.DMA
    result = pltpu.VMEM((QUOTA, SIDE, SIDE), F32)
    operands = (chaos_field, mean_field, kl_fields, pattern, coupling, slot_mode.reshape(1, SLOTS))
    operands = [pltpu.with_memory_space_constraint(operand, pltpu.HBM) for operand in operands]
    own, far = pl.pallas_call(
        kernel,
        out_shape=(result, result),
        in_specs=[pl.BlockSpec(memory_space=pltpu.HBM)] * len(operands),
        out_specs=(pl.BlockSpec(memory_space=pl.ANY),) * 2,
        scratch_shapes=[
            pltpu.VMEM((QUOTA, SIDE, SIDE), F32),
            pltpu.VMEM((SIDE + 2, PAD, SIDE), F32),
            pltpu.VMEM((TERMS, SIDE + 2 * ROWS, SIDE), F32),
            pltpu.VMEM((TERMS, SLOTS, SLOTS), jnp.int32),
            pltpu.VMEM((TERMS, SLOTS, SLOTS), F32),
            pltpu.VMEM((1, SLOTS), jnp.int32),
            pltpu.VMEM((3, 2 * MIXED, DEPTH), BF16),
            pltpu.VMEM((3, DEPTH, DENSE), BF16),
            pltpu.VMEM((2, CHUNKS, QUOTA, ROWS, SIDE), F32),
            pltpu.VMEM((2, CHUNKS, TERMS, ROWS, SIDE), F32),
            pltpu.VMEM((2, 7, TERMS, ROWS, SIDE), F32),
            pltpu.VMEM((ROWS, MIXED, SIDE), F32),
            pltpu.VMEM((CHUNKS, GROUPS, QUOTA, ROWS, SIDE), F32),
            pltpu.VMEM((EARLY, 2, QUOTA, ROWS, SIDE), F32),
            pltpu.VMEM((GATHERED, GROUPS, QUOTA, ROWS, SIDE), F32),
            pltpu.VMEM((GATHERED * ROWS + 1, DENSE, SIDE), BF16),
            pltpu.VMEM((2, ROWS + 2, DEPTH, SIDE), F32),
            pltpu.VMEM((QUOTA, LATE * ROWS, SIDE), F32),
            dma((6,)),
            dma((CHUNKS,)),
            dma,
            dma((3, GATHERED)),
            dma((3, GATHERED)),
            dma((PAIRS,)),
            dma((PAIRS,)),
            dma((2, CHUNKS)),
            dma((2, CHUNKS)),
            dma((2, PAIRS)),
            dma((2, PAIRS)),
            dma((2, PAIRS)),
            dma((2, PAIRS)),
            dma((2, CHUNKS)),
            dma((2, CHUNKS)),
            dma((CHUNKS,)),
            dma((CHUNKS,)),
        ],
        compiler_params=pltpu.CompilerParams(
            collective_id=0, has_side_effects=True, vmem_limit_bytes=48 << 20
        ),
    )(*operands)
    return (own + far).reshape(QUOTA, 1, SIDE, SIDE)


def solution(mesh):
    in_specs = (
        P("mode", "space", None, None),
        P("space", None, None),
        P(None, "space", None, None),
        P(),
        P(),
        P(),
    )
    out_specs = P("mode", "space", None, None)
    return jax.shard_map(
        on_device, mesh=mesh, in_specs=in_specs, out_specs=out_specs, check_vma=False
    )
```
